32 devices in a mesh: groups: 2 (over y), leaf: 4 (over z), rep: 4 (over x, core).
Axes of the slice: x: 2, y: 2, z: 4, core: 2. Of those that a mesh axis runs over, the one named last changes fastest.
Arguments:
- start_point: float32 [1024, 192], P(('groups', 'leaf', 'rep')), parts along dimension 0, may hold values from -6 to 6
- start_residual: float32 [1024, 192], P(('groups', 'leaf', 'rep')), parts along dimension 0, may hold values from -6 to 6
- leaf_order: int32 [1024], P(('groups', 'leaf', 'rep')), parts along dimension 0, may hold values from 0 to 511, as said below
- leaf_padding: int32 [1024], P(('groups', 'leaf', 'rep')), parts along dimension 0, may hold values from 0 to 16
- point_coords: float32 [1024, 192], P(('groups', 'leaf', 'rep')), parts along dimension 0, may hold values from 0 to 1
- point_weights: float32 [1024, 64], P(('groups', 'leaf', 'rep')), parts along dimension 0, may hold values from 0.005 to 0.05
- leaf_basis: float32 [1024, 32, 192], P(('groups', 'leaf', 'rep')), parts along dimension 0, may hold values from -0.4375 to 0.4375
- transfer_one: float32 [1024, 32, 32], P(('groups', 'leaf', 'rep')), parts along dimension 0, may hold values from -1 to 1
- transfer_two: float32 [512, 32, 32], P(('groups', 'leaf', 'rep')), parts along dimension 0, may hold values from -1 to 1
- couple_leaf: int32 [1024, 8], P(('groups', 'leaf', 'rep')), parts along dimension 0, may hold values from 0 to 511, as said below
- couple_pair: int32 [512, 8], P(('groups', 'leaf', 'rep')), parts along dimension 0, may hold values from 0 to 255, as said below
- couple_quad: int32 [256, 8], P(('groups', 'leaf', 'rep')), parts along dimension 0, may hold values from 0 to 127, as said below
- coupling_leaf: float32 [1024, 8, 32, 32], P(('groups', 'leaf', 'rep')), parts along dimension 0, may hold values from -1 to 1
- coupling_pair: float32 [512, 8, 32, 32], P(('groups', 'leaf', 'rep')), parts along dimension 0, may hold values from -1 to 1
- coupling_quad: float32 [256, 8, 32, 32], P(('groups', 'leaf', 'rep')), parts along dimension 0, may hold values from -1 to 1
- near_lists: int32 [1024, 6], P(('groups', 'leaf', 'rep')), parts along dimension 0, may hold values from 0 to 511, as said below
Outputs:
- next_point: float32 [1024, 192], P(('groups', 'leaf', 'rep')), parts along dimension 0
- next_residual: float32 [1024, 192], P(('groups', 'leaf', 'rep')), parts along dimension 0
The draws below stay inside these ranges and needn't reach their ends.
There are 2 independent parts, one for each index of `groups`. The reference program is written for one: setup_inputs(seed, part) draws one part's arguments, and reference() takes and returns one part's arrays. A program takes and returns all parts, laid end to end along the dimension named above; each array names one. Nothing has to cross between parts.
Inputs may be any that keep to these rules, and one draw needn't show every extreme that they name: `leaf_order`: A permutation. The blocks of one device (rows of one device in partition order) go to leaves of devices with the same rep index; one device hands either none or exactly 16 of its blocks to leaves of any one device. `near_lists`: entry 0 of row g is g. Every entry lies in subtree g // 128 or in the subtree just before or after it. `couple_leaf`: every entry of row t lies in subtree t // 128 or in the subtree just before or after it. `couple_pair`: every entry of row t names a pair in subtree 2 * t // 128 or in the subtree just before or after it (pair c lies in subtree 2 * c // 128). `couple_quad`: every entry of row t names a quad in subtree 4 * t // 128 or in the subtree just before or after it (quad c lies in subtree 4 * c // 128).
All inputs are finite; a program needn't handle non-finite values.
Results may differ from the reference program's by a relative error of at most 0.00005.
Values sent between devices are 32-bit elements; how exact they have to be, the bound alone decides.
No kernel may reach another device: no remote copies, remote signals or barrier semaphores. Data moves between devices by JAX's collectives and lax.ppermute only.
A program may use at most 64 MiB of HBM per device.

```python
import math
import jax
import jax.numpy as jnp
from jax import lax

PTS = 64
LW = 192
RANK = 32
NEAR = 6
COUP = 8
LEAF_DEV = 32
LEAF_SUB = 128
NL = 512
CAP = 16


def nearby_entries(key, row_total, per_subtree, columns):
    first_key, second_key = jax.random.split(key)
    subtrees = row_total // per_subtree
    row_index = jnp.arange(row_total, dtype=jnp.int32)
    home_subtree = row_index // per_subtree
    moved = jax.random.randint(first_key, (row_total, columns), -1, 2, dtype=jnp.int32)
    target_subtree = jnp.clip(home_subtree[:, None] + moved, 0, subtrees - 1)
    inside = jax.random.randint(second_key, (row_total, columns), 0, per_subtree, dtype=jnp.int32)
    return target_subtree * per_subtree + inside


def draw_near_lists(key, part):
    key = jax.random.fold_in(key, 11)
    entries = nearby_entries(key, NL, LEAF_SUB, NEAR)
    return entries.at[:, 0].set(jnp.arange(NL, dtype=jnp.int32))


def draw_couple_leaf(key, part):
    key = jax.random.fold_in(key, 12)
    return nearby_entries(key, NL, LEAF_SUB, COUP)


def draw_couple_pair(key, part):
    key = jax.random.fold_in(key, 13)
    return nearby_entries(key, NL // 2, LEAF_SUB // 2, COUP)


def draw_couple_quad(key, part):
    key = jax.random.fold_in(key, 14)
    return nearby_entries(key, NL // 4, LEAF_SUB // 4, COUP)


def draw_leaf_order(key, part):
    key = jax.random.fold_in(key, 15)
    first_key, second_key, third_key = jax.random.split(key, 3)
    devices = NL // LEAF_DEV
    subtrees = NL // LEAF_SUB
    members = LEAF_SUB // LEAF_DEV
    start_perm = jax.vmap(lambda sub_key: jax.random.permutation(sub_key, subtrees))(jax.random.split(first_key, members)).astype(jnp.int32)
    target_perm = jax.vmap(lambda sub_key: jax.random.permutation(sub_key, subtrees))(jax.random.split(second_key, members)).astype(jnp.int32)
    within = jax.vmap(lambda sub_key: jax.random.permutation(sub_key, LEAF_DEV))(jax.random.split(third_key, devices)).astype(jnp.int32)
    blocks = jnp.arange(NL, dtype=jnp.int32)
    device = blocks // LEAF_DEV
    home_subtree = device // members
    member = device % members
    slot_index = blocks % LEAF_DEV
    group_index = slot_index // CAP
    target_subtree = target_perm[member, (start_perm[member, home_subtree] + group_index) % subtrees]
    target_device = target_subtree * members + member
    return target_device * LEAF_DEV + within[target_device, slot_index]


def place_ends(values, rng, low, high):
    longest = values.shape.index(max(values.shape))
    spots = []
    for shift in (0, 1):
        where = [jax.random.randint(jax.random.fold_in(rng, axis), (), 0, length) for axis, length in enumerate(values.shape)]
        where[longest] = (where[longest] + shift) % values.shape[longest]
        spots.append(tuple(where))
    return values.at[spots[0]].set(low).at[spots[1]].set(high)


def steps_of(own_key, extent, shards, low, largest):
    factor_of, own = 1.0, jax.random.fold_in(own_key, 6)
    for position, blocks in shards:
        heights = jnp.exp(jax.random.uniform(jax.random.fold_in(own, position), (blocks,), jnp.float32, low / len(shards), largest / len(shards)))
        factor_of = factor_of * jnp.repeat(heights, extent[position] // blocks).reshape([-1 if axis == position else 1 for axis in range(len(extent))])
    return factor_of


def normal_values(own_key, dims, deviation, reach, cuts=(), held_as=jnp.bfloat16):
    loudness = steps_of(own_key, dims, cuts, -0.22, 0.18) if cuts else 1.0
    drawn = jax.random.normal(own_key, dims, jnp.float32) * deviation * loudness
    return jnp.minimum(jnp.maximum(drawn, -reach), reach).astype(held_as)


def setup_inputs(seed: int = 0, part: int = 0) -> dict:
    arg_keys = jax.random.split(jax.random.key(seed), 17)
    part_splits = jax.random.split(jax.random.fold_in(arg_keys[16], part), 17)
    return {
        "start_point": normal_values(part_splits[0], (NL, LW), 1.0, 6.0, ((0, 16),), jnp.float32),
        "start_residual": normal_values(part_splits[1], (NL, LW), 1.0, 6.0, ((0, 16),), jnp.float32),
        "leaf_order": draw_leaf_order(jax.random.fold_in(jax.random.fold_in(arg_keys[16], part), 71), part),
        "leaf_padding": place_ends(jax.random.randint(part_splits[3], (NL,), 0, 17), jax.random.fold_in(part_splits[3], 1), 0, 16).astype(jnp.int32),
        "point_coords": jnp.clip(1.0 * jax.random.uniform(part_splits[4], (NL, LW), jnp.float32) ** steps_of(part_splits[4], (NL, LW), ((0, 16),), -0.2, 0.2), 0.0, 1.0),
        "point_weights": jnp.clip(jnp.exp(math.log(0.05) - 2.3025851 * jax.random.uniform(part_splits[5], (NL, PTS), jnp.float32) ** steps_of(part_splits[5], (NL, PTS), ((0, 16),), -0.2, 0.2)), 0.005, 0.05),
        "leaf_basis": normal_values(part_splits[6], (NL, RANK, LW), LW ** -0.5, 0.4375, ((0, 16),), jnp.float32),
        "transfer_one": normal_values(part_splits[7], (NL, RANK, RANK), RANK ** -0.5, 1.0, ((0, 16),), jnp.float32),
        "transfer_two": normal_values(part_splits[8], (NL // 2, RANK, RANK), RANK ** -0.5, 1.0, ((0, 16),), jnp.float32),
        "couple_leaf": draw_couple_leaf(jax.random.fold_in(jax.random.fold_in(arg_keys[16], part), 71), part),
        "couple_pair": draw_couple_pair(jax.random.fold_in(jax.random.fold_in(arg_keys[16], part), 71), part),
        "couple_quad": draw_couple_quad(jax.random.fold_in(jax.random.fold_in(arg_keys[16], part), 71), part),
        "coupling_leaf": normal_values(part_splits[12], (NL, COUP, RANK, RANK), RANK ** -0.5, 1.0, ((0, 16),), jnp.float32),
        "coupling_pair": normal_values(part_splits[13], (NL // 2, COUP, RANK, RANK), RANK ** -0.5, 1.0, ((0, 16),), jnp.float32),
        "coupling_quad": normal_values(part_splits[14], (NL // 4, COUP, RANK, RANK), RANK ** -0.5, 1.0, ((0, 16),), jnp.float32),
        "near_lists": draw_near_lists(jax.random.fold_in(jax.random.fold_in(arg_keys[16], part), 71), part),
    }


PRECISE = lax.Precision.HIGHEST
JUMP = 0.5
SMOOTH_SQUARE = 0.01
KELVIN_DIAG = 2.2
KELVIN_DIRECT = 1.0
EPSILON = 1e-06

def kelvin_block(target_coords, source_coords, source_load):
    offset = target_coords[:, :, :, None] - source_coords[:, :, None, :]
    radius_square = lax.optimization_barrier(jnp.sum(offset * offset, axis=1)) + SMOOTH_SQUARE
    inverse = lax.rsqrt(radius_square)
    along_sum = lax.optimization_barrier(jnp.sum(offset * source_load[:, :, None, :], axis=1))
    direct = jnp.einsum('bps,bas->bap', inverse, source_load, precision=PRECISE)
    cubic_term = jnp.einsum('baps,bps->bap', offset, inverse * inverse * inverse * along_sum, precision=PRECISE)
    return KELVIN_DIAG * direct + KELVIN_DIRECT * cubic_term

def spread_sources(source_table, near_rows):
    leaves, near_count = near_rows.shape
    points = source_table.shape[1] // 3
    picked = source_table[near_rows].reshape(leaves, near_count, 3, points)
    return picked.transpose(0, 2, 1, 3).reshape(leaves, 3, near_count * points)

def reference(start_point, start_residual, leaf_order, leaf_padding, point_coords, point_weights, leaf_basis, transfer_one, transfer_two, couple_leaf, couple_pair, couple_quad, coupling_leaf, coupling_pair, coupling_quad, near_lists):
    point_live = (jnp.arange(PTS, dtype=jnp.int32)[None, :] < (PTS - leaf_padding)[:, None]).astype(jnp.float32)
    point_mask = jnp.tile(point_live, (1, 3))
    load_weight = point_weights * point_live
    target_coords = point_coords.reshape(NL, 3, PTS)
    source_coords = spread_sources(point_coords, near_lists)
    source_weight = load_weight[near_lists].reshape(NL, NEAR * PTS)
    block_size = min(64, NL)
    block_total = NL // block_size

    def apply_operator(vector):
        subtree_vector = jnp.zeros_like(vector).at[leaf_order].set(vector)
        masked = point_mask * subtree_vector
        source_load = spread_sources(masked, near_lists) * source_weight[:, None, :]
        near_pieces = lax.map(lambda pieces: kelvin_block(*pieces), (target_coords.reshape(block_total, block_size, 3, PTS), source_coords.reshape(block_total, block_size, 3, NEAR * PTS), source_load.reshape(block_total, block_size, 3, NEAR * PTS)))
        near_field = near_pieces.reshape(NL, LW)
        expansion_leaf = jnp.einsum('gip,gp->gi', leaf_basis, masked, precision=PRECISE)
        expansion_pair = jnp.einsum('gij,gj->gi', transfer_one, expansion_leaf, precision=PRECISE).reshape(NL // 2, 2, RANK).sum(axis=1)
        expansion_quad = jnp.einsum('gij,gj->gi', transfer_two, expansion_pair, precision=PRECISE).reshape(NL // 4, 2, RANK).sum(axis=1)
        field_leaf = jnp.einsum('tkij,tkj->ti', coupling_leaf, expansion_leaf[couple_leaf], precision=PRECISE)
        field_pair = jnp.einsum('tkij,tkj->ti', coupling_pair, expansion_pair[couple_pair], precision=PRECISE)
        field_quad = jnp.einsum('tkij,tkj->ti', coupling_quad, expansion_quad[couple_quad], precision=PRECISE)
        total_pair = field_pair + jnp.einsum('cij,ci->cj', transfer_two, jnp.repeat(field_quad, 2, axis=0), precision=PRECISE)
        total_leaf = field_leaf + jnp.einsum('gij,gi->gj', transfer_one, jnp.repeat(total_pair, 2, axis=0), precision=PRECISE)
        far_field = jnp.einsum('gip,gi->gp', leaf_basis, total_leaf, precision=PRECISE)
        image_subtree = point_mask * (JUMP * masked + near_field + far_field) + (1.0 - point_mask) * subtree_vector
        return image_subtree[leaf_order]
    scale_norm = jnp.sqrt(jnp.sum(start_residual * start_residual) + EPSILON)
    basis_zero = start_residual / scale_norm
    image_zero = apply_operator(basis_zero)
    top_first = jnp.sum(basis_zero * image_zero)
    remainder = image_zero - top_first * basis_zero
    below_first = jnp.sqrt(jnp.sum(remainder * remainder) + EPSILON)
    basis_one = remainder / below_first
    image_one = apply_operator(basis_one)
    top_second = jnp.sum(basis_zero * image_one)
    mid_second = jnp.sum(basis_one * image_one)
    leftover = image_one - top_second * basis_zero - mid_second * basis_one
    below_second = jnp.sqrt(jnp.sum(leftover * leftover) + EPSILON)
    gram_first = top_first * top_first + below_first * below_first
    gram_cross = top_first * top_second + below_first * mid_second
    gram_second = top_second * top_second + mid_second * mid_second + below_second * below_second
    determinant = gram_first * gram_second - gram_cross * gram_cross
    step_zero = scale_norm * (gram_second * top_first - gram_cross * top_second) / determinant
    step_one = scale_norm * (gram_first * top_second - gram_cross * top_first) / determinant
    next_point = start_point + step_zero * basis_zero + step_one * basis_one
    next_residual = start_residual - step_zero * image_zero - step_one * image_one
    return (next_point, next_residual)
```

```python
import functools

import jax
import jax.numpy as jnp
from jax import lax
from jax.experimental import pallas as pl
from jax.experimental.pallas import tpu as pltpu
from jax.sharding import PartitionSpec as P

PRECISE = lax.Precision.HIGHEST
JUMP = 0.5
SMOOTH_SQUARE = 0.01
KELVIN_DIAG = 2.2
EPSILON = 1e-06
LANES = 128
VMEM_LIMIT = 56 * 1024 * 1024


def lane_ids(rows):
    return lax.broadcasted_iota(jnp.int32, (rows, LANES), 1)


def columns_of(rows, count, column):
    lanes = lane_ids(rows)
    table = jnp.zeros((rows, LANES), jnp.float32)
    for g in range(count):
        table = jnp.where(lanes == g, column(g), table)
    return table


def lane_sum(value):
    return jnp.sum(value, axis=1, keepdims=True)


def expansions(masked, basis_ref, one_ref, two_ref):
    leaves, rank = basis_ref.shape[0], basis_ref.shape[1]
    leaf_columns = columns_of(rank, leaves, lambda g: lane_sum(basis_ref[g] * masked[g : g + 1, :]))
    leaf_rows = leaf_columns.T[:leaves, :]
    pair_columns = columns_of(
        rank,
        leaves // 2,
        lambda c: lane_sum(
            one_ref[2 * c] * leaf_rows[2 * c : 2 * c + 1, :]
            + one_ref[2 * c + 1] * leaf_rows[2 * c + 1 : 2 * c + 2, :]
        ),
    )
    pair_rows = pair_columns.T[: leaves // 2, :]
    quad_columns = columns_of(
        rank,
        leaves // 4,
        lambda c: lane_sum(
            two_ref[2 * c] * pair_rows[2 * c : 2 * c + 1, :]
            + two_ref[2 * c + 1] * pair_rows[2 * c + 1 : 2 * c + 2, :]
        ),
    )
    quad_rows = quad_columns.T[: leaves // 4, :]
    rest = jnp.zeros((leaves - leaves // 2 - leaves // 4, rank), jnp.float32)
    upper = jnp.concatenate([pair_rows, quad_rows, rest], axis=0)
    return jnp.concatenate([leaf_rows, upper], axis=1)


def order_kernel(leaf_total, base_ref, *refs):
    shards = refs[:leaf_total]
    mask_ref, coords_ref, weight_ref, basis_ref, one_ref, two_ref, out_ref, vector_ref = refs[leaf_total:]
    leaves, width = mask_ref.shape
    rows = jnp.concatenate([shard[...] for shard in shards], axis=0)
    place = rows[:, width : width + 1] - base_ref[0].astype(jnp.float32)
    ids = lax.broadcasted_iota(jnp.int32, (rows.shape[0], leaves), 1).astype(jnp.float32)
    pick = (place == ids).astype(jnp.float32)
    vector = lax.dot_general(
        pick, rows, (((0,), (0,)), ((), ())), precision=PRECISE, preferred_element_type=jnp.float32
    )[:, :width]
    vector_ref[...] = vector
    spread = expansions(mask_ref[...] * vector, basis_ref, one_ref, two_ref)
    out_ref[...] = jnp.concatenate([vector, spread, coords_ref[...], weight_ref[...]], axis=1)


def build_tables(geometry, vector, tables):
    x_ref, y_ref, z_ref, u0_ref, u1_ref, u2_ref, leaf_ref, upper_ref = tables
    low = lane_ids(geometry.shape[0]) < 64
    swap = lambda v: pltpu.roll(v, 64, 1)
    first, second = geometry[:, :LANES], geometry[:, LANES:]
    first_swap, second_swap = swap(first), swap(second)
    x_ref[...] = jnp.where(low, first, first_swap)
    y_ref[...] = jnp.where(low, first_swap, first)
    z_ref[...] = jnp.where(low, second, second_swap)
    weight = jnp.where(low, second_swap, second)
    head, tail = vector[:, :LANES], vector[:, LANES:]
    head_swap, tail_swap = swap(head), swap(tail)
    u0_ref[...] = jnp.where(low, head, head_swap) * weight
    u1_ref[...] = jnp.where(low, head_swap, head) * weight
    u2_ref[...] = jnp.where(low, tail, tail_swap) * weight
    leaf_ref[...] = tail_swap
    upper_ref[...] = pltpu.roll(tail, 32, 1)


def near_field(near_ref, target_ref, tables, out_ref):
    leaves, near_count = near_ref.shape
    points = target_ref.shape[1] // 3
    low = lane_ids(8) < 64
    lanes = lane_ids(8)
    out_ref[...] = jnp.zeros_like(out_ref)

    def leaf_step(g, carry):
        sources = []
        for k in range(0, near_count, 2):
            one, other = near_ref[g, k], near_ref[g, k + 1]
            values = [
                jnp.where(
                    low,
                    jnp.broadcast_to(ref[pl.ds(one, 1), :], (8, LANES)),
                    jnp.broadcast_to(ref[pl.ds(other, 1), :], (8, LANES)),
                )
                for ref in tables[:6]
            ]
            sources.append(values + [KELVIN_DIAG * u for u in values[3:]])
        for p in range(0, points, 8):
            tx, ty, tz = [target_ref[g, a * points + p : a * points + p + 8, :] for a in range(3)]
            sums = None
            for x, y, z, u0, u1, u2, k0, k1, k2 in sources:
                dx, dy, dz = tx - x, ty - y, tz - z
                inverse = lax.rsqrt(dx * dx + dy * dy + (dz * dz + SMOOTH_SQUARE))
                along = dx * u0 + dy * u1 + dz * u2
                cubic = (inverse * inverse) * (inverse * along)
                terms = [inverse * k0 + cubic * dx, inverse * k1 + cubic * dy, inverse * k2 + cubic * dz]
                sums = terms if sums is None else [s + t for s, t in zip(sums, terms)]
            for a in range(3):
                rows = pl.ds(a * points + p, 8)
                out_ref[rows, :] = jnp.where(lanes == g, lane_sum(sums[a]), out_ref[rows, :])
        return carry

    lax.fori_loop(0, leaves, leaf_step, 0)


def coupled(lists_ref, matrix_ref, table_ref, field_ref):
    count, partners = lists_ref.shape
    rank = matrix_ref.shape[2]
    lanes = lane_ids(rank)
    step = 4

    def cluster_step(s, field):
        for u in range(step):
            t = s * step + u
            total = None
            for k in range(partners):
                row = table_ref[pl.ds(lists_ref[t, k], 1), :][:, :rank]
                term = matrix_ref[t, k] * row
                total = term if total is None else total + term
            field = jnp.where(lanes == t, lane_sum(total), field)
        return field

    field_ref[...] = lax.fori_loop(0, count // step, cluster_step, jnp.zeros((rank, LANES), jnp.float32))


def rows_of(columns, matrix_ref, share):
    count = matrix_ref.shape[0]
    rows = []
    for c in range(count):
        column = columns[:, c // share : c // share + 1]
        rows.append(jnp.sum(matrix_ref[c] * column, axis=0, keepdims=True))
    return jnp.concatenate(rows, axis=0)


def columns_from_rows(rows):
    count, width = rows.shape
    padded = jnp.concatenate([rows, jnp.zeros((count, LANES - width), jnp.float32)], axis=1)
    full = jnp.concatenate([padded, jnp.zeros((LANES - count, LANES), jnp.float32)], axis=0)
    return full.T[:width, :]


def operator(own, mask, refs, tables, scratch):
    near_ref, leaf_list, pair_list, quad_list, target_ref, basis_ref, one_ref, two_ref, c_leaf, c_pair, c_quad = refs
    near_out, f_leaf, f_pair, f_quad = scratch
    leaves, width = own.shape
    coupled(quad_list, c_quad, tables[7], f_quad)
    coupled(pair_list, c_pair, tables[7], f_pair)
    coupled(leaf_list, c_leaf, tables[6], f_leaf)
    total_pair = f_pair[...] + columns_from_rows(rows_of(f_quad[...], two_ref, 2))
    total_leaf = f_leaf[...] + columns_from_rows(rows_of(total_pair, one_ref, 2))
    far = rows_of(total_leaf, basis_ref, 1)
    near_field(near_ref, target_ref, tables, near_out)
    near = near_out[...].T[:leaves, :]
    return mask * (JUMP * (mask * own) + near + far) + (1.0 - mask) * own


def total_of(value):
    return jnp.sum(jnp.sum(value, axis=1, keepdims=True), axis=0, keepdims=True)


def in_lanes(values):
    lanes = lax.broadcasted_iota(jnp.int32, (8, 2 * LANES), 1)
    table = jnp.zeros((8, 2 * LANES), jnp.float32)
    for g, value in enumerate(values):
        table = jnp.where(lanes == g, value, table)
    return table


def first_kernel(*refs):
    lists, (gathered_ref, own_ref, mask_ref), arrays = refs[:4], refs[4:7], refs[7:14]
    out_ref = refs[14]
    tables, scratch = refs[15:23], refs[23:27]
    gathered = gathered_ref[...]
    build_tables(gathered[:, 256:], gathered[:, :256], tables)
    own, mask = own_ref[...], mask_ref[...]
    image = operator(own, mask, lists + arrays, tables, scratch)
    leaves = own.shape[0]
    spread = expansions(mask * image, *arrays[1:4])
    out_ref[0:leaves, :] = jnp.concatenate([image, spread], axis=1)
    out_ref[leaves : leaves + 8, :] = in_lanes([total_of(own * own), total_of(own * image)])


def second_kernel(reps, *refs):
    lists, (gathered_ref, later_ref, own_ref, image_ref, mask_ref), arrays = refs[:4], refs[4:9], refs[9:16]
    out_ref, global_ref = refs[16:18]
    tables, scratch = refs[18:26], refs[26:30]
    own, mask = own_ref[...], mask_ref[...]
    leaves, width = own.shape
    span = gathered_ref.shape[0] // reps
    sums = sum(later_ref[i * (span + 8) + span : i * (span + 8) + span + 8, :] for i in range(reps))
    global_ref[...] = sums
    top = sums[0:1, 1:2] / (sums[0:1, 0:1] + EPSILON)
    vector = jnp.concatenate(
        [
            later_ref[i * (span + 8) : i * (span + 8) + span, :] - top * gathered_ref[i * span : (i + 1) * span, :256]
            for i in range(reps)
        ],
        axis=0,
    )
    build_tables(gathered_ref[:, 256:], vector, tables)
    rest = image_ref[0:leaves, :width] - top * own
    image = operator(rest, mask, lists + arrays, tables, scratch)
    out_ref[0:leaves, :] = jnp.concatenate([image, jnp.zeros((leaves, 2 * LANES - width), jnp.float32)], axis=1)
    out_ref[leaves : leaves + 8, :] = in_lanes(
        [total_of(rest * rest), total_of(own * image), total_of(rest * image), total_of(image * image)]
    )


def pick_kernel(leaf_total, slot_ref, *refs):
    first, second = refs[:leaf_total], refs[leaf_total : 2 * leaf_total]
    first_out, second_out = refs[2 * leaf_total :]
    leaves, width = first_out.shape
    ids = lax.broadcasted_iota(jnp.int32, (leaves, leaf_total * leaves), 1)
    pick = (slot_ref[...] == ids).astype(jnp.float32)
    for shards, out in ((first, first_out), (second, second_out)):
        rows = jnp.concatenate([shard[0:leaves, :] for shard in shards], axis=0)
        out[...] = jnp.dot(pick, rows, precision=PRECISE, preferred_element_type=jnp.float32)[:, :width]


def finish_kernel(point_ref, residual_ref, first_ref, second_ref, global_ref, sums_ref, next_point, next_residual):
    at = lambda ref, j: ref[0:1, j : j + 1]
    scale_square = at(global_ref, 0) + EPSILON
    scale = jnp.sqrt(scale_square)
    norm = at(global_ref, 0) / scale_square
    top_first = at(global_ref, 1) / scale_square
    rest_square = at(sums_ref, 0) / scale_square
    below_square = rest_square + EPSILON
    below_first = jnp.sqrt(below_square)
    top_second = at(sums_ref, 1) / (scale_square * below_first)
    mid_second = at(sums_ref, 2) / (scale_square * below_square)
    image_square = at(sums_ref, 3) / (scale_square * below_square)
    one_square = rest_square / below_square
    cross = (top_first - top_first * norm) / below_first
    below_second_square = (
        image_square
        - 2.0 * top_second * top_second
        - 2.0 * mid_second * mid_second
        + top_second * top_second * norm
        + mid_second * mid_second * one_square
        + 2.0 * top_second * mid_second * cross
        + EPSILON
    )
    gram_first = top_first * top_first + below_square
    gram_cross = top_first * top_second + below_first * mid_second
    gram_second = top_second * top_second + mid_second * mid_second + below_second_square
    determinant = gram_first * gram_second - gram_cross * gram_cross
    step_zero = scale * (gram_second * top_first - gram_cross * top_second) / determinant
    step_one = scale * (gram_first * top_second - gram_cross * top_first) / determinant
    residual, first, second = residual_ref[...], first_ref[...], second_ref[...]
    inverse = 1.0 / (scale * below_first)
    rest = first - top_first * residual
    along_zero = step_zero / scale
    along_one = step_one * inverse
    next_point[...] = point_ref[...] + along_zero * residual + along_one * rest
    next_residual[...] = residual - along_zero * first - along_one * second


def body(
    start_point,
    start_residual,
    leaf_order,
    leaf_padding,
    point_coords,
    point_weights,
    leaf_basis,
    transfer_one,
    transfer_two,
    couple_leaf,
    couple_pair,
    couple_quad,
    coupling_leaf,
    coupling_pair,
    coupling_quad,
    near_lists,
):
    leaves, width = start_point.shape
    points = point_weights.shape[1]
    rank = leaf_basis.shape[1]
    leaf_total = lax.axis_size("leaf")
    reps = lax.axis_size("rep")
    leaf_index = lax.axis_index("leaf")
    rep_index = lax.axis_index("rep")
    f32 = jnp.float32
    vmem = pl.BlockSpec(memory_space=pltpu.VMEM)
    smem = pl.BlockSpec(memory_space=pltpu.SMEM)
    params = pltpu.CompilerParams(vmem_limit_bytes=VMEM_LIMIT)

    def shifted(value, shift):
        pairs = [(i, (i + shift) % leaf_total) for i in range(leaf_total)]
        return lax.ppermute(value, "leaf", pairs)

    def around(value):
        return [value] + [shifted(value, shift) for shift in range(1, leaf_total)]

    point_live = jnp.arange(points, dtype=jnp.int32)[None, :] < (points - leaf_padding)[:, None]
    point_live = point_live.astype(f32)
    point_mask = jnp.tile(point_live, (1, 3))
    load_weight = point_weights * point_live

    def rows(lists, per_device, offset):
        owner = lists // per_device
        place = (owner % reps) * 3 + owner // reps - (leaf_index - 1)
        return place * leaves + lists % per_device + offset

    lists = (
        rows(near_lists, leaves, 0),
        rows(couple_leaf, leaves, 0),
        rows(couple_pair, leaves // 2, 0),
        rows(couple_quad, leaves // 4, leaves // 2),
    )
    targets = jnp.broadcast_to(point_coords[:, :, None], (leaves, width, LANES))
    arrays = (targets, leaf_basis, transfer_one, transfer_two, coupling_leaf, coupling_pair, coupling_quad)
    home = leaf_order // (leaves * reps)
    slots = ((leaf_index - home) % leaf_total) * leaves + leaf_order % leaves

    order_column = jnp.broadcast_to(leaf_order.astype(f32)[:, None], (leaves, 2 * LANES - width))
    ordered = around(jnp.concatenate([start_residual, order_column], axis=1))
    base = ((leaf_index * reps + rep_index) * leaves).astype(jnp.int32).reshape(1)
    payload, own = pl.pallas_call(
        functools.partial(order_kernel, leaf_total),
        out_shape=(
            jax.ShapeDtypeStruct((leaves, 4 * LANES), f32),
            jax.ShapeDtypeStruct((leaves, width), f32),
        ),
        in_specs=[smem] + [vmem] * (leaf_total + 6),
        out_specs=(vmem, vmem),
        compiler_params=params,
        name="order",
    )(base, *ordered, point_mask, point_coords, load_weight, leaf_basis, transfer_one, transfer_two)
    before, after = shifted(payload, 1), shifted(payload, leaf_total - 1)
    gathered = lax.all_gather(jnp.concatenate([before, payload, after], axis=0), "rep", axis=0, tiled=True)
    table_rows = gathered.shape[0]
    scratch = [pltpu.VMEM((table_rows, LANES), f32)] * 8 + [pltpu.VMEM((width, LANES), f32)]
    scratch = scratch + [pltpu.VMEM((rank, LANES), f32)] * 3
    first = pl.pallas_call(
        first_kernel,
        out_shape=jax.ShapeDtypeStruct((leaves + 8, 2 * LANES), f32),
        in_specs=[smem] * 4 + [vmem] * 10,
        out_specs=vmem,
        scratch_shapes=scratch,
        compiler_params=params,
        name="first",
    )(*lists, gathered, own, point_mask, *arrays)
    firsts = around(first)
    sums = sum(shard[leaves:] for shard in firsts)
    later = lax.all_gather(
        jnp.concatenate([firsts[1][:leaves], first[:leaves], firsts[leaf_total - 1][:leaves], sums], axis=0),
        "rep",
        axis=0,
        tiled=True,
    )
    second, global_sums = pl.pallas_call(
        functools.partial(second_kernel, reps),
        out_shape=(
            jax.ShapeDtypeStruct((leaves + 8, 2 * LANES), f32),
            jax.ShapeDtypeStruct((8, 2 * LANES), f32),
        ),
        in_specs=[smem] * 4 + [vmem] * 12,
        out_specs=(vmem, vmem),
        scratch_shapes=scratch,
        compiler_params=params,
        name="second",
    )(*lists, gathered, later, own, first, point_mask, *arrays)
    seconds = around(second)
    last = sum(shard[leaves:] for shard in seconds)
    step = 1
    while step < reps:
        last = last + lax.ppermute(last, "rep", [(i, i ^ step) for i in range(reps)])
        step *= 2
    first_image, second_image = pl.pallas_call(
        functools.partial(pick_kernel, leaf_total),
        out_shape=(jax.ShapeDtypeStruct((leaves, width), f32),) * 2,
        in_specs=[vmem] * (1 + 2 * leaf_total),
        out_specs=(vmem, vmem),
        compiler_params=params,
        name="pick",
    )(slots[:, None], *firsts, *seconds)
    return pl.pallas_call(
        finish_kernel,
        out_shape=(jax.ShapeDtypeStruct((leaves, width), f32),) * 2,
        in_specs=[vmem] * 6,
        out_specs=(vmem, vmem),
        compiler_params=params,
        name="finish",
    )(start_point, start_residual, first_image, second_image, global_sums, last)


def solution(mesh):
    line = P(("groups", "leaf", "rep"))
    two = P(("groups", "leaf", "rep"), None)
    three = P(("groups", "leaf", "rep"), None, None)
    four = P(("groups", "leaf", "rep"), None, None, None)
    placed = (two, two, line, line, two, two, three, three, three, two, two, two, four, four, four, two)
    return jax.shard_map(body, mesh=mesh, in_specs=placed, out_specs=(two, two), check_vma=False)
```

```python
import functools

import jax
import jax.numpy as jnp
from jax import lax
from jax.experimental import pallas as pl
from jax.experimental.pallas import tpu as pltpu
from jax.sharding import PartitionSpec as P

PRECISE = lax.Precision.HIGHEST
JUMP = 0.5
SMOOTH_SQUARE = 0.01
KELVIN_DIAG = 2.2
EPSILON = 1e-06
LANES = 128
VMEM_LIMIT = 60 * 1024 * 1024


def lane_ids(rows):
    return lax.broadcasted_iota(jnp.int32, (rows, LANES), 1)


def columns_of(rows, count, column):
    lanes = lane_ids(rows)
    table = jnp.zeros((rows, LANES), jnp.float32)
    for g in range(count):
        table = jnp.where(lanes == g, column(g), table)
    return table


def lane_sum(value):
    return jnp.sum(value, axis=1, keepdims=True)


def expansions(masked, basis_ref, one_ref, two_ref):
    leaves, rank = basis_ref.shape[0], basis_ref.shape[1]
    leaf_columns = columns_of(rank, leaves, lambda g: lane_sum(basis_ref[g] * masked[g : g + 1, :]))
    leaf_rows = leaf_columns.T[:leaves, :]
    pair_columns = columns_of(
        rank,
        leaves // 2,
        lambda c: lane_sum(
            one_ref[2 * c] * leaf_rows[2 * c : 2 * c + 1, :]
            + one_ref[2 * c + 1] * leaf_rows[2 * c + 1 : 2 * c + 2, :]
        ),
    )
    pair_rows = pair_columns.T[: leaves // 2, :]
    quad_columns = columns_of(
        rank,
        leaves // 4,
        lambda c: lane_sum(
            two_ref[2 * c] * pair_rows[2 * c : 2 * c + 1, :]
            + two_ref[2 * c + 1] * pair_rows[2 * c + 1 : 2 * c + 2, :]
        ),
    )
    quad_rows = quad_columns.T[: leaves // 4, :]
    rest = jnp.zeros((leaves - leaves // 2 - leaves // 4, rank), jnp.float32)
    upper = jnp.concatenate([pair_rows, quad_rows, rest], axis=0)
    return jnp.concatenate([leaf_rows, upper], axis=1)


def start_copies(sources, targets, sems):
    copies = [pltpu.make_async_copy(x, y, sems.at[i]) for i, (x, y) in enumerate(zip(sources, targets))]
    for copy in copies:
        copy.start()
    return copies


def order_kernel(leaf_total, reps, bases_ref, *refs):
    shards = refs[:leaf_total]
    coords_ref, weight_ref, *raw_lists = refs[leaf_total : leaf_total + 6]
    sources, (out_ref, vector_ref, mask_ref, lists_ref) = refs[leaf_total + 6 : -8], refs[-8:-4]
    basis_ref, one_ref, two_ref, sems = refs[-4:]
    copies = start_copies(sources, (basis_ref, one_ref, two_ref), sems)
    leaves, width = vector_ref.shape
    leaf_index, rep_index = bases_ref[leaf_total], bases_ref[leaf_total + 1]
    lists_ref[...] = jnp.zeros_like(lists_ref)
    for i, raw in enumerate(raw_lists):
        entries = raw[...]
        height = max(i - 1, 0)
        bits = (leaves >> height).bit_length() - 1
        owner = entries >> bits
        turned = (owner >> (reps.bit_length() - 1)) ^ leaf_index
        place = ((owner & (reps - 1)) ^ rep_index) * 3 + jnp.where(turned > 1, 2, turned)
        row = place * leaves + (entries & ((1 << bits) - 1)) + (leaves // 2 if i == 3 else 0)
        lists_ref[8 * i : 8 * i + row.shape[0], 0 : row.shape[1]] = row
    points = weight_ref.shape[1]
    base = bases_ref[0].astype(jnp.float32)
    ids = lax.broadcasted_iota(jnp.int32, (leaves, leaves), 0)
    places = base + ids.astype(jnp.float32)
    vector = None
    for shard in shards:
        pick = (shard[leaves : leaves + 1, :leaves] == places).astype(jnp.float32)
        part = jnp.dot(pick, shard[0:leaves, :], precision=PRECISE, preferred_element_type=jnp.float32)
        vector = part if vector is None else vector + part
    same = ids == lax.broadcasted_iota(jnp.int32, (leaves, leaves), 1)
    padding = lane_sum(jnp.where(same, shards[0][leaves + 1 : leaves + 2, :leaves], 0.0))
    point = lax.broadcasted_iota(jnp.int32, (leaves, width), 1) & (points - 1)
    mask = (point.astype(jnp.float32) < points - padding).astype(jnp.float32)
    mask_ref[...] = mask
    vector_ref[...] = vector
    for copy in copies:
        copy.wait()
    spread = expansions(mask * vector, basis_ref, one_ref, two_ref)
    weight = weight_ref[...] * mask[:, :points]
    out_ref[...] = jnp.concatenate([vector, spread, coords_ref[...], weight], axis=1)


def build_tables(place, geometry, vector, tables):
    rows = pl.ds(place * geometry.shape[0], geometry.shape[0])
    x_ref, y_ref, z_ref, u0_ref, u1_ref, u2_ref, leaf_ref, upper_ref = [ref.at[rows, :] for ref in tables]
    low = lane_ids(geometry.shape[0]) < 64
    swap = lambda v: pltpu.roll(v, 64, 1)
    first, second = geometry[:, :LANES], geometry[:, LANES:]
    first_swap, second_swap = swap(first), swap(second)
    x_ref[...] = jnp.where(low, first, first_swap)
    y_ref[...] = jnp.where(low, first_swap, first)
    z_ref[...] = jnp.where(low, second, second_swap)
    weight = jnp.where(low, second_swap, second)
    head, tail = vector[:, :LANES], vector[:, LANES:]
    head_swap, tail_swap = swap(head), swap(tail)
    u0_ref[...] = jnp.where(low, head, head_swap) * weight
    u1_ref[...] = jnp.where(low, head_swap, head) * weight
    u2_ref[...] = jnp.where(low, tail, tail_swap) * weight
    leaf_ref[...] = tail_swap
    upper_ref[...] = pltpu.roll(tail, 32, 1)


def near_field(lists_ref, near_count, target_ref, tables, out_ref):
    leaves, points = target_ref.shape[0], target_ref.shape[1] // 3
    low = lane_ids(8) < 64
    lanes = lane_ids(8)
    out_ref[...] = jnp.zeros_like(out_ref)

    def leaf_field(g):
        sources = []
        for k in range(0, near_count, 2):
            one, other = lists_ref[k, g], lists_ref[k + 1, g]
            values = [
                jnp.where(
                    low,
                    jnp.broadcast_to(ref[pl.ds(one, 1), :], (8, LANES)),
                    jnp.broadcast_to(ref[pl.ds(other, 1), :], (8, LANES)),
                )
                for ref in tables[:6]
            ]
            sources.append(values + [KELVIN_DIAG * u for u in values[3:]])
        for p in range(0, points, 8):
            tx, ty, tz = [target_ref[g, a * points + p : a * points + p + 8, :] for a in range(3)]
            sums = None
            for x, y, z, u0, u1, u2, k0, k1, k2 in sources:
                dx, dy, dz = tx - x, ty - y, tz - z
                inverse = lax.rsqrt(dx * dx + dy * dy + (dz * dz + SMOOTH_SQUARE))
                along = dx * u0 + dy * u1 + dz * u2
                cubic = (inverse * inverse) * (inverse * along)
                terms = [inverse * k0 + cubic * dx, inverse * k1 + cubic * dy, inverse * k2 + cubic * dz]
                sums = terms if sums is None else [s + t for s, t in zip(sums, terms)]
            for a in range(3):
                rows = pl.ds(a * points + p, 8)
                out_ref[rows, :] = jnp.where(lanes == g, lane_sum(sums[a]), out_ref[rows, :])

    def some_leaves(step, carry):
        for u in range(4):
            leaf_field(step * 4 + u)
        return carry

    lax.fori_loop(0, leaves // 4, some_leaves, 0)


def coupled(entry, matrix_ref, table_ref, field_ref):
    count, partners, rank = matrix_ref.shape[:3]
    lanes = lane_ids(rank)
    step = 4

    def cluster_step(s, field):
        for u in range(step):
            t = s * step + u
            total = None
            for k in range(partners):
                row = table_ref[pl.ds(entry(t, k), 1), :][:, :rank]
                term = matrix_ref[t, k] * row
                total = term if total is None else total + term
            field = jnp.where(lanes == t, lane_sum(total), field)
        return field

    field_ref[...] = lax.fori_loop(0, count // step, cluster_step, jnp.zeros((rank, LANES), jnp.float32))


def rows_of(columns, matrix_ref, share):
    count = matrix_ref.shape[0]
    rows = []
    for c in range(count):
        column = columns[:, c // share : c // share + 1]
        rows.append(jnp.sum(matrix_ref[c] * column, axis=0, keepdims=True))
    return jnp.concatenate(rows, axis=0)


def columns_from_rows(rows):
    count, width = rows.shape
    padded = jnp.concatenate([rows, jnp.zeros((count, LANES - width), jnp.float32)], axis=1)
    full = jnp.concatenate([padded, jnp.zeros((LANES - count, LANES), jnp.float32)], axis=0)
    return full.T[:width, :]


def fill_targets(coords, target_ref):
    leaves, width = coords.shape
    padded = jnp.concatenate([coords, jnp.zeros((LANES - leaves, width), jnp.float32)], axis=0)
    columns = padded.T
    for g in range(leaves):
        target_ref[g] = jnp.broadcast_to(columns[:, g : g + 1], (width, LANES))


def operator(own, mask, lists_ref, near_count, copies, held, tables, scratch):
    basis_ref, one_ref, two_ref, c_leaf, c_pair, c_quad = held
    target_ref, near_out, f_leaf, f_pair, f_quad = scratch
    leaves = own.shape[0]
    near_field(lists_ref, near_count, target_ref, tables, near_out)
    for copy in copies:
        copy.wait()
    coupled(lambda t, k: lists_ref[24 + t, k], c_quad, tables[7], f_quad)
    coupled(lambda t, k: lists_ref[16 + k, t], c_pair, tables[7], f_pair)
    coupled(lambda t, k: lists_ref[8 + k, t], c_leaf, tables[6], f_leaf)
    total_pair = f_pair[...] + columns_from_rows(rows_of(f_quad[...], two_ref, 2))
    total_leaf = f_leaf[...] + columns_from_rows(rows_of(total_pair, one_ref, 2))
    far = rows_of(total_leaf, basis_ref, 1)
    near = near_out[...].T[:leaves, :]
    return mask * (JUMP * (mask * own) + near + far) + (1.0 - mask) * own


def total_of(value):
    return jnp.sum(jnp.sum(value, axis=1, keepdims=True), axis=0, keepdims=True)


def in_lanes(values):
    lanes = lax.broadcasted_iota(jnp.int32, (8, 2 * LANES), 1)
    table = jnp.zeros((8, 2 * LANES), jnp.float32)
    for g, value in enumerate(values):
        table = jnp.where(lanes == g, value, table)
    return table


def first_kernel(reps, near_count, lists_ref, *refs):
    gathered, (own_ref, mask_ref, coords_ref), sources = refs[:reps], refs[reps : reps + 3], refs[reps + 3 : reps + 9]
    out_ref, sems = refs[reps + 9 : reps + 11]
    held, tables, scratch = refs[reps + 11 : reps + 17], refs[reps + 17 : reps + 25], refs[reps + 25 :]
    copies = start_copies(sources, held, sems)
    fill_targets(coords_ref[...], scratch[0])
    for i in range(reps):
        build_tables(i, gathered[i][:, 256:], gathered[i][:, :256], tables)
    own, mask = own_ref[...], mask_ref[...]
    image = operator(own, mask, lists_ref, near_count, copies, held, tables, scratch)
    spread = expansions(mask * image, *held[:3])
    out_ref[...] = jnp.concatenate([image, spread], axis=1)


def second_kernel(reps, near_count, lists_ref, *refs):
    gathered, later, refs = refs[:reps], refs[reps : 2 * reps], refs[2 * reps :]
    residual_ref, own_ref, mask_ref, coords_ref = refs[:4]
    sources, (out_ref, sems) = refs[4:10], refs[10:12]
    held, tables, scratch = refs[12:18], refs[18:26], refs[26:]
    copies = start_copies(sources, held, sems)
    fill_targets(coords_ref[...], scratch[0])
    for i in range(reps):
        build_tables(i, gathered[i][:, 256:], later[i][...], tables)
    residual, mask = residual_ref[...], mask_ref[...]
    leaves, width = residual.shape
    own = own_ref[:, :width]
    image = operator(own, mask, lists_ref, near_count, copies, held, tables, scratch)
    out_ref[0:leaves, :] = jnp.concatenate([image, jnp.zeros((leaves, 2 * LANES - width), jnp.float32)], axis=1)
    pairs = ((residual, residual), (residual, own), (own, own), (residual, image), (own, image), (image, image))
    out_ref[leaves : leaves + 8, :] = in_lanes([total_of(x * y) for x, y in pairs])


def pick_kernel(leaf_total, bases_ref, order_ref, *refs):
    first, second = refs[:leaf_total], refs[leaf_total : 2 * leaf_total]
    outs = refs[2 * leaf_total :]
    leaves, width = outs[0].shape
    order = order_ref[leaves : leaves + 1, :leaves]
    ids = lax.broadcasted_iota(jnp.int32, (leaves, leaves), 0).astype(jnp.float32)
    totals = [None, None]
    for k in range(leaf_total):
        pick = (order == ids + bases_ref[k].astype(jnp.float32)).astype(jnp.float32)
        for i, shard in enumerate((first[k], second[k])):
            part = lax.dot_general(
                pick,
                shard[0:leaves, :],
                (((0,), (0,)), ((), ())),
                precision=PRECISE,
                preferred_element_type=jnp.float32,
            )
            totals[i] = part if totals[i] is None else totals[i] + part
    for total, out in zip(totals, outs):
        out[...] = total[:, :width]


def finish_kernel(point_ref, residual_ref, first_ref, second_ref, *refs):
    next_point, next_residual = refs[-2:]
    sums = sum(ref[...] for ref in refs[:-2])
    rr, rw, ww, rv, wv, vv = [sums[0:1, j : j + 1] for j in range(6)]
    scale_square = rr + EPSILON
    scale = jnp.sqrt(scale_square)
    norm = rr / scale_square
    top_first = rw / scale_square
    rest_square = (ww - 2.0 * top_first * rw + top_first * top_first * rr) / scale_square
    along_image = (rv - top_first * rw) / scale_square
    rest_image = (wv - top_first * ww - top_first * (rv - top_first * rw)) / scale_square
    image_square = (vv - 2.0 * top_first * wv + top_first * top_first * ww) / scale_square
    rest_square = jnp.maximum(rest_square, 0.0)
    below_square = rest_square + EPSILON
    below_first = jnp.sqrt(below_square)
    top_second = along_image / below_first
    mid_second = rest_image / below_square
    image_square = image_square / below_square
    one_square = rest_square / below_square
    cross = (top_first - top_first * norm) / below_first
    below_second_square = (
        image_square
        - 2.0 * top_second * top_second
        - 2.0 * mid_second * mid_second
        + top_second * top_second * norm
        + mid_second * mid_second * one_square
        + 2.0 * top_second * mid_second * cross
        + EPSILON
    )
    gram_first = top_first * top_first + below_square
    gram_cross = top_first * top_second + below_first * mid_second
    gram_second = top_second * top_second + mid_second * mid_second + below_second_square
    determinant = gram_first * gram_second - gram_cross * gram_cross
    step_zero = scale * (gram_second * top_first - gram_cross * top_second) / determinant
    step_one = scale * (gram_first * top_second - gram_cross * top_first) / determinant
    residual, first = residual_ref[...], first_ref[...]
    rest = first - top_first * residual
    rest_image = second_ref[...] - top_first * first
    along_zero = step_zero / scale
    along_one = step_one / (scale * below_first)
    next_point[...] = point_ref[...] + along_zero * residual + along_one * rest
    next_residual[...] = residual - along_zero * first - along_one * rest_image


def body(
    start_point,
    start_residual,
    leaf_order,
    leaf_padding,
    point_coords,
    point_weights,
    leaf_basis,
    transfer_one,
    transfer_two,
    couple_leaf,
    couple_pair,
    couple_quad,
    coupling_leaf,
    coupling_pair,
    coupling_quad,
    near_lists,
):
    leaves, width = start_point.shape
    points = point_weights.shape[1]
    rank = leaf_basis.shape[1]
    leaf_total = lax.axis_size("leaf")
    reps = lax.axis_size("rep")
    leaf_index = lax.axis_index("leaf")
    rep_index = lax.axis_index("rep")
    f32 = jnp.float32
    vmem = pl.BlockSpec(memory_space=pltpu.VMEM)
    smem = pl.BlockSpec(memory_space=pltpu.SMEM)
    hbm = pl.BlockSpec(memory_space=pltpu.HBM)
    params = pltpu.CompilerParams(vmem_limit_bytes=VMEM_LIMIT)
    small = pltpu.CompilerParams(vmem_limit_bytes=VMEM_LIMIT // 4)

    def facing(value, turn):
        return lax.ppermute(value, "leaf", [(i, i ^ turn) for i in range(leaf_total)])

    def beside(value):
        other = [min(max(((i + 1) ^ 1) - 1, 0), leaf_total - 1) for i in range(leaf_total)]
        return lax.ppermute(value, "leaf", list(enumerate(other)))

    def around(value):
        return [value] + [facing(value, turn) for turn in range(1, leaf_total)]

    def crossed(value, step):
        return lax.ppermute(value, "rep", [(i, i ^ step) for i in range(reps)])

    def members(value):
        found = [value]
        for k in range(1, reps):
            found.append(crossed(found[k - 1], 1) if k % 2 else crossed(value, k))
        return found

    near_count = near_lists.shape[1]
    homes = leaf_index ^ jnp.arange(leaf_total, dtype=jnp.int32)
    bases = jnp.concatenate([(homes * reps + rep_index) * leaves, jnp.stack([leaf_index, rep_index])]).astype(jnp.int32)
    raw_lists = (near_lists.T, couple_leaf.T, couple_pair.T, couple_quad)

    numbers = jnp.pad(jnp.stack([leaf_order, leaf_padding]).astype(f32), ((0, 6), (0, width - leaves)))
    ordered = around(jnp.concatenate([start_residual, numbers], axis=0))
    up = (leaf_basis, transfer_one, transfer_two)
    matrices = up + (coupling_leaf, coupling_pair, coupling_quad)
    room = lambda arrays: [pltpu.SemaphoreType.DMA((len(arrays),))] + [pltpu.VMEM(m.shape, f32) for m in arrays]
    payload, own, mask, lists = pl.pallas_call(
        functools.partial(order_kernel, leaf_total, reps),
        out_shape=(jax.ShapeDtypeStruct((leaves, 4 * LANES), f32),)
        + (jax.ShapeDtypeStruct((leaves, width), f32),) * 2
        + (jax.ShapeDtypeStruct((32, leaves), jnp.int32),),
        in_specs=[smem] + [vmem] * (leaf_total + 6) + [hbm] * 3,
        out_specs=(vmem,) * 4,
        scratch_shapes=room(up)[1:] + room(up)[:1],
        compiler_params=params,
        name="order",
    )(bases, *ordered, point_coords, point_weights, *raw_lists, *up)
    gathered = members(jnp.concatenate([payload, facing(payload, 1), beside(payload)], axis=0))
    scratch = room(matrices) + [pltpu.VMEM((3 * leaves * reps, LANES), f32)] * 8
    scratch = scratch + [pltpu.VMEM((leaves, width, LANES), f32), pltpu.VMEM((width, LANES), f32)]
    scratch = scratch + [pltpu.VMEM((rank, LANES), f32)] * 3
    first = pl.pallas_call(
        functools.partial(first_kernel, reps, near_count),
        out_shape=jax.ShapeDtypeStruct((leaves, 2 * LANES), f32),
        in_specs=[smem] + [vmem] * (reps + 3) + [hbm] * 6,
        out_specs=vmem,
        scratch_shapes=scratch,
        compiler_params=params,
        name="first",
    )(lists, *gathered, own, mask, point_coords, *matrices)
    first_facing = facing(first, 1)
    later = members(jnp.concatenate([first, first_facing, beside(first)], axis=0))
    firsts = [first, first_facing] + [facing(first, turn) for turn in range(2, leaf_total)]
    second = pl.pallas_call(
        functools.partial(second_kernel, reps, near_count),
        out_shape=jax.ShapeDtypeStruct((leaves + 8, 2 * LANES), f32),
        in_specs=[smem] + [vmem] * (2 * reps + 4) + [hbm] * 6,
        out_specs=vmem,
        scratch_shapes=scratch,
        compiler_params=params,
        name="second",
    )(lists, *gathered, *later, own, first, mask, point_coords, *matrices)
    seconds = around(second)
    last = sum(shard[leaves:] for shard in seconds)
    lasts = [last] + [crossed(last, k) for k in range(1, reps)]
    first_image, second_image = pl.pallas_call(
        functools.partial(pick_kernel, leaf_total),
        out_shape=(jax.ShapeDtypeStruct((leaves, width), f32),) * 2,
        in_specs=[smem] + [vmem] * (1 + 2 * leaf_total),
        out_specs=(vmem, vmem),
        compiler_params=small,
        name="pick",
    )(bases, ordered[0], *firsts, *seconds)
    return pl.pallas_call(
        finish_kernel,
        out_shape=(jax.ShapeDtypeStruct((leaves, width), f32),) * 2,
        in_specs=[vmem] * (4 + reps),
        out_specs=(vmem, vmem),
        compiler_params=small,
        name="finish",
    )(start_point, start_residual, first_image, second_image, *lasts)


def solution(mesh):
    line = P(("groups", "leaf", "rep"))
    two = P(("groups", "leaf", "rep"), None)
    three = P(("groups", "leaf", "rep"), None, None)
    four = P(("groups", "leaf", "rep"), None, None, None)
    placed = (two, two, line, line, two, two, three, three, three, two, two, two, four, four, four, two)
    return jax.shard_map(body, mesh=mesh, in_specs=placed, out_specs=(two, two), check_vma=False)
```

```python
import functools

import jax
import jax.numpy as jnp
from jax import lax
from jax.experimental import pallas as pl
from jax.experimental.pallas import tpu as pltpu
from jax.sharding import PartitionSpec as P

PRECISE = lax.Precision.HIGHEST
JUMP = 0.5
SMOOTH_SQUARE = 0.01
KELVIN_DIAG = 2.2
EPSILON = 1e-06
LANES = 128
VMEM_LIMIT = 60 * 1024 * 1024


def lane_ids(rows):
    return lax.broadcasted_iota(jnp.int32, (rows, LANES), 1)


def columns_of(rows, count, column):
    lanes = lane_ids(rows)
    table = jnp.zeros((rows, LANES), jnp.float32)
    for g in range(count):
        table = jnp.where(lanes == g, column(g), table)
    return table


def lane_sum(value):
    return jnp.sum(value, axis=1, keepdims=True)


def expansions(masked, basis_ref, one_ref, two_ref):
    leaves, rank = basis_ref.shape[0], basis_ref.shape[1]
    leaf_columns = columns_of(rank, leaves, lambda g: lane_sum(basis_ref[g] * masked[g : g + 1, :]))
    leaf_rows = leaf_columns.T[:leaves, :]
    pair_columns = columns_of(
        rank,
        leaves // 2,
        lambda c: lane_sum(
            one_ref[2 * c] * leaf_rows[2 * c : 2 * c + 1, :]
            + one_ref[2 * c + 1] * leaf_rows[2 * c + 1 : 2 * c + 2, :]
        ),
    )
    pair_rows = pair_columns.T[: leaves // 2, :]
    quad_columns = columns_of(
        rank,
        leaves // 4,
        lambda c: lane_sum(
            two_ref[2 * c] * pair_rows[2 * c : 2 * c + 1, :]
            + two_ref[2 * c + 1] * pair_rows[2 * c + 1 : 2 * c + 2, :]
        ),
    )
    quad_rows = quad_columns.T[: leaves // 4, :]
    rest = jnp.zeros((leaves - leaves // 2 - leaves // 4, rank), jnp.float32)
    upper = jnp.concatenate([pair_rows, quad_rows, rest], axis=0)
    return jnp.concatenate([leaf_rows, upper], axis=1)


def start_copies(sources, targets, sems):
    copies = [pltpu.make_async_copy(x, y, sems.at[i]) for i, (x, y) in enumerate(zip(sources, targets))]
    for copy in copies:
        copy.start()
    return copies


def exact_dot(left, right, dims=((1,), (0,))):
    return lax.dot_general(left, right, (dims, ((), ())), precision=PRECISE, preferred_element_type=jnp.float32)


def send_kernel(leaf_total, bits, order_ref, residual_ref, slots_ref, *outs):
    leaves, width = residual_ref.shape
    capacity = outs[0].shape[0]
    order = order_ref[...]
    turned = (order >> bits) ^ lax.axis_index("leaf")
    ids = lax.broadcasted_iota(jnp.int32, (8 * ((leaf_total + 7) // 8), leaves), 0)
    mine = (turned == ids).astype(jnp.float32)
    row, column = [lax.broadcasted_iota(jnp.int32, (leaves, leaves), i) for i in (0, 1)]
    rank = exact_dot(mine, (row < column).astype(jnp.float32))
    slot = lax.broadcasted_iota(jnp.int32, (capacity, leaves), 0).astype(jnp.float32)
    position = ((order & (leaves - 1)) + 1).astype(jnp.float32)
    slots = jnp.concatenate(
        [jnp.where(slot == rank[k : k + 1, :], mine[k : k + 1, :], 0.0) for k in range(leaf_total)], axis=0
    )
    slots_ref[...] = slots
    rows = exact_dot(slots, residual_ref[...])
    place = jnp.broadcast_to(lane_sum(slots * position), (leaf_total * capacity, 2 * LANES - width))
    payload = jnp.concatenate([rows, place], axis=1)
    for k in range(leaf_total):
        outs[k][...] = payload[k * capacity : (k + 1) * capacity, :]


def order_kernel(leaf_total, reps, *refs):
    shards = refs[:leaf_total]
    padding_ref, coords_ref, weight_ref, *raw_lists = refs[leaf_total : leaf_total + 7]
    sources, (out_ref, vector_ref, mask_ref, lists_ref, arrive_ref) = refs[leaf_total + 7 : -9], refs[-9:-4]
    basis_ref, one_ref, two_ref, sems = refs[-4:]
    copies = start_copies(sources, (basis_ref, one_ref, two_ref), sems)
    leaves, width = vector_ref.shape
    leaf_index, rep_index = lax.axis_index("leaf"), lax.axis_index("rep")
    lists_ref[...] = jnp.zeros_like(lists_ref)
    for i, raw in enumerate(raw_lists):
        entries = raw[...]
        height = max(i - 1, 0)
        bits = (leaves >> height).bit_length() - 1
        owner = entries >> bits
        turned = (owner >> (reps.bit_length() - 1)) ^ leaf_index
        place = ((owner & (reps - 1)) ^ rep_index) * 3 + jnp.where(turned > 1, 2, turned)
        row = place * leaves + (entries & ((1 << bits) - 1)) + (leaves // 2 if i == 3 else 0)
        lists_ref[8 * i : 8 * i + row.shape[0], 0 : row.shape[1]] = row
    points = weight_ref.shape[1]
    rows = jnp.concatenate([shard[...] for shard in shards], axis=0)
    ids = lax.broadcasted_iota(jnp.int32, (rows.shape[0], leaves), 1) + 1
    arrive = (rows[:, width : width + 1] == ids.astype(jnp.float32)).astype(jnp.float32)
    arrive_ref[...] = arrive
    vector = exact_dot(arrive, rows, ((0,), (0,)))[:, :width]
    row, column = [lax.broadcasted_iota(jnp.int32, (leaves, leaves), i) for i in (0, 1)]
    padding = lane_sum(jnp.where(row == column, padding_ref[...].astype(jnp.float32), 0.0))
    point = lax.broadcasted_iota(jnp.int32, (leaves, width), 1) & (points - 1)
    mask = (point.astype(jnp.float32) < points - padding).astype(jnp.float32)
    mask_ref[...] = mask
    vector_ref[...] = vector
    for copy in copies:
        copy.wait()
    spread = expansions(mask * vector, basis_ref, one_ref, two_ref)
    weight = weight_ref[...] * mask[:, :points]
    out_ref[...] = jnp.concatenate([vector, spread, coords_ref[...], weight], axis=1)


def build_tables(place, geometry, vector, tables):
    rows = pl.ds(place * geometry.shape[0], geometry.shape[0])
    x_ref, y_ref, z_ref, u0_ref, u1_ref, u2_ref, leaf_ref, upper_ref = [ref.at[rows, :] for ref in tables]
    low = lane_ids(geometry.shape[0]) < 64
    swap = lambda v: pltpu.roll(v, 64, 1)
    first, second = geometry[:, :LANES], geometry[:, LANES:]
    first_swap, second_swap = swap(first), swap(second)
    x_ref[...] = jnp.where(low, first, first_swap)
    y_ref[...] = jnp.where(low, first_swap, first)
    z_ref[...] = jnp.where(low, second, second_swap)
    weight = jnp.where(low, second_swap, second)
    head, tail = vector[:, :LANES], vector[:, LANES:]
    head_swap, tail_swap = swap(head), swap(tail)
    u0_ref[...] = jnp.where(low, head, head_swap) * weight
    u1_ref[...] = jnp.where(low, head_swap, head) * weight
    u2_ref[...] = jnp.where(low, tail, tail_swap) * weight
    leaf_ref[...] = tail_swap
    upper_ref[...] = pltpu.roll(tail, 32, 1)


def near_field(lists_ref, near_count, target_ref, tables, out_ref):
    leaves, points = target_ref.shape[0], target_ref.shape[1] // 3
    low = lane_ids(8) < 64
    lanes = lane_ids(8)
    out_ref[...] = jnp.zeros_like(out_ref)

    def leaf_field(g):
        sources = []
        for k in range(0, near_count, 2):
            one, other = lists_ref[k, g], lists_ref[k + 1, g]
            values = [
                jnp.where(
                    low,
                    jnp.broadcast_to(ref[pl.ds(one, 1), :], (8, LANES)),
                    jnp.broadcast_to(ref[pl.ds(other, 1), :], (8, LANES)),
                )
                for ref in tables[:6]
            ]
            sources.append(values)
        for p in range(0, points, 8):
            tx, ty, tz = [target_ref[g, a * points + p : a * points + p + 8, :] for a in range(3)]
            direct = bent = None
            for x, y, z, u0, u1, u2 in sources:
                dx, dy, dz = tx - x, ty - y, tz - z
                inverse = lax.rsqrt(dx * dx + dy * dy + (dz * dz + SMOOTH_SQUARE))
                along = dx * u0 + dy * u1 + dz * u2
                cubic = (inverse * inverse) * (inverse * along)
                terms = [inverse * u0, inverse * u1, inverse * u2], [cubic * dx, cubic * dy, cubic * dz]
                direct = terms[0] if direct is None else [s + t for s, t in zip(direct, terms[0])]
                bent = terms[1] if bent is None else [s + t for s, t in zip(bent, terms[1])]
            sums = [KELVIN_DIAG * s + t for s, t in zip(direct, bent)]
            for a in range(3):
                rows = pl.ds(a * points + p, 8)
                out_ref[rows, :] = jnp.where(lanes == g, lane_sum(sums[a]), out_ref[rows, :])

    def some_leaves(step, carry):
        for u in range(8):
            leaf_field(step * 8 + u)
        return carry

    lax.fori_loop(0, leaves // 8, some_leaves, 0)


def coupled(entry, matrix_ref, table_ref, field_ref):
    count, partners, rank = matrix_ref.shape[:3]
    lanes = lane_ids(rank)
    step = 8

    def cluster_step(s, field):
        for u in range(step):
            t = s * step + u
            total = None
            for k in range(partners):
                row = table_ref[pl.ds(entry(t, k), 1), :][:, :rank]
                term = matrix_ref[t, k] * row
                total = term if total is None else total + term
            field = jnp.where(lanes == t, lane_sum(total), field)
        return field

    field_ref[...] = lax.fori_loop(0, count // step, cluster_step, jnp.zeros((rank, LANES), jnp.float32))


def rows_of(columns, matrix_ref, share):
    count = matrix_ref.shape[0]
    rows = []
    for c in range(count):
        column = columns[:, c // share : c // share + 1]
        rows.append(jnp.sum(matrix_ref[c] * column, axis=0, keepdims=True))
    return jnp.concatenate(rows, axis=0)


def columns_from_rows(rows):
    count, width = rows.shape
    padded = jnp.concatenate([rows, jnp.zeros((count, LANES - width), jnp.float32)], axis=1)
    full = jnp.concatenate([padded, jnp.zeros((LANES - count, LANES), jnp.float32)], axis=0)
    return full.T[:width, :]


def fill_targets(coords, target_ref):
    leaves, width = coords.shape
    padded = jnp.concatenate([coords, jnp.zeros((LANES - leaves, width), jnp.float32)], axis=0)
    columns = padded.T
    for g in range(leaves):
        target_ref[g] = jnp.broadcast_to(columns[:, g : g + 1], (width, LANES))


def operator(own, mask, lists_ref, near_count, copies, held, tables, scratch):
    basis_ref, one_ref, two_ref, c_leaf, c_pair, c_quad = held
    target_ref, near_out, f_leaf, f_pair, f_quad = scratch
    leaves = own.shape[0]
    near_field(lists_ref, near_count, target_ref, tables, near_out)
    for copy in copies:
        copy.wait()
    coupled(lambda t, k: lists_ref[24 + t, k], c_quad, tables[7], f_quad)
    coupled(lambda t, k: lists_ref[16 + k, t], c_pair, tables[7], f_pair)
    coupled(lambda t, k: lists_ref[8 + k, t], c_leaf, tables[6], f_leaf)
    total_pair = f_pair[...] + columns_from_rows(rows_of(f_quad[...], two_ref, 2))
    total_leaf = f_leaf[...] + columns_from_rows(rows_of(total_pair, one_ref, 2))
    far = rows_of(total_leaf, basis_ref, 1)
    near = near_out[...].T[:leaves, :]
    return mask * (JUMP * (mask * own) + near + far) + (1.0 - mask) * own


def total_of(value):
    return jnp.sum(jnp.sum(value, axis=1, keepdims=True), axis=0, keepdims=True)


def in_lanes(values):
    lanes = lane_ids(8)
    table = jnp.zeros((8, LANES), jnp.float32)
    for g, value in enumerate(values):
        table = jnp.where(lanes == g, value, table)
    return table


def first_kernel(reps, near_count, lists_ref, *refs):
    gathered, (own_ref, mask_ref, coords_ref), sources = refs[:reps], refs[reps : reps + 3], refs[reps + 3 : reps + 9]
    out_ref, sems = refs[reps + 9 : reps + 11]
    held, tables, scratch = refs[reps + 11 : reps + 17], refs[reps + 17 : reps + 25], refs[reps + 25 :]
    copies = start_copies(sources, held, sems)
    fill_targets(coords_ref[...], scratch[0])
    for i in range(reps):
        build_tables(i, gathered[i][:, 256:], gathered[i][:, :256], tables)
    own, mask = own_ref[...], mask_ref[...]
    image = operator(own, mask, lists_ref, near_count, copies, held, tables, scratch)
    spread = expansions(mask * image, *held[:3])
    out_ref[...] = jnp.concatenate([image, spread], axis=1)


def second_kernel(reps, near_count, lists_ref, *refs):
    gathered, later, refs = refs[:reps], refs[reps : 2 * reps], refs[2 * reps :]
    residual_ref, own_ref, mask_ref, coords_ref, arrive_ref = refs[:5]
    sources, outs, sems = refs[5:11], refs[11:-20], refs[-20]
    held, tables, scratch = refs[-19:-13], refs[-13:-5], refs[-5:]
    copies = start_copies(sources, held, sems)
    fill_targets(coords_ref[...], scratch[0])
    for i in range(reps):
        build_tables(i, gathered[i][:, 256:], later[i][...], tables)
    residual, mask = residual_ref[...], mask_ref[...]
    width = residual.shape[1]
    own = own_ref[:, :width]
    image = operator(own, mask, lists_ref, near_count, copies, held, tables, scratch)
    pairs = ((residual, residual), (residual, own), (own, own), (residual, image), (own, image), (image, image))
    sums = in_lanes([total_of(x * y) for x, y in pairs])
    capacity = outs[0].shape[0]
    if capacity > 8:
        sums = jnp.concatenate([sums, jnp.zeros((capacity - 8, LANES), jnp.float32)], axis=0)
    rows = exact_dot(arrive_ref[...], jnp.concatenate([image, own], axis=1))
    for k, out_ref in enumerate(outs):
        out_ref[...] = jnp.concatenate([rows[k * capacity : (k + 1) * capacity, :], sums], axis=1)


def pick_kernel(slots_ref, *refs):
    shards, (second_ref, first_ref) = refs[:-2], refs[-2:]
    width = first_ref.shape[1]
    rows = jnp.concatenate([shard[...] for shard in shards], axis=0)
    found = exact_dot(slots_ref[...], rows[:, : 2 * width], ((0,), (0,)))
    second_ref[...] = found[:, :width]
    first_ref[...] = found[:, width:]


def finish_kernel(point_ref, residual_ref, first_ref, second_ref, *refs):
    next_point, next_residual = refs[-2:]
    sums = sum(ref[...] for ref in refs[:-2])
    rr, rw, ww, rv, wv, vv = [sums[0:1, j : j + 1] for j in range(6)]
    scale_square = rr + EPSILON
    scale = jnp.sqrt(scale_square)
    norm = rr / scale_square
    top_first = rw / scale_square
    rest_square = (ww - 2.0 * top_first * rw + top_first * top_first * rr) / scale_square
    along_image = (rv - top_first * rw) / scale_square
    rest_image = (wv - top_first * ww - top_first * (rv - top_first * rw)) / scale_square
    image_square = (vv - 2.0 * top_first * wv + top_first * top_first * ww) / scale_square
    rest_square = jnp.maximum(rest_square, 0.0)
    below_square = rest_square + EPSILON
    below_first = jnp.sqrt(below_square)
    top_second = along_image / below_first
    mid_second = rest_image / below_square
    image_square = image_square / below_square
    one_square = rest_square / below_square
    cross = (top_first - top_first * norm) / below_first
    below_second_square = (
        image_square
        - 2.0 * top_second * top_second
        - 2.0 * mid_second * mid_second
        + top_second * top_second * norm
        + mid_second * mid_second * one_square
        + 2.0 * top_second * mid_second * cross
        + EPSILON
    )
    gram_first = top_first * top_first + below_square
    gram_cross = top_first * top_second + below_first * mid_second
    gram_second = top_second * top_second + mid_second * mid_second + below_second_square
    determinant = gram_first * gram_second - gram_cross * gram_cross
    step_zero = scale * (gram_second * top_first - gram_cross * top_second) / determinant
    step_one = scale * (gram_first * top_second - gram_cross * top_first) / determinant
    residual, first = residual_ref[...], first_ref[...]
    rest = first - top_first * residual
    rest_image = second_ref[...] - top_first * first
    along_zero = step_zero / scale
    along_one = step_one / (scale * below_first)
    next_point[...] = point_ref[...] + along_zero * residual + along_one * rest
    next_residual[...] = residual - along_zero * first - along_one * rest_image


def body(
    start_point,
    start_residual,
    leaf_order,
    leaf_padding,
    point_coords,
    point_weights,
    leaf_basis,
    transfer_one,
    transfer_two,
    couple_leaf,
    couple_pair,
    couple_quad,
    coupling_leaf,
    coupling_pair,
    coupling_quad,
    near_lists,
):
    leaves, width = start_point.shape
    points = point_weights.shape[1]
    rank = leaf_basis.shape[1]
    leaf_total = lax.axis_size("leaf")
    reps = lax.axis_size("rep")
    f32 = jnp.float32
    vmem = pl.BlockSpec(memory_space=pltpu.VMEM)
    smem = pl.BlockSpec(memory_space=pltpu.SMEM)
    hbm = pl.BlockSpec(memory_space=pltpu.HBM)
    params = pltpu.CompilerParams(vmem_limit_bytes=VMEM_LIMIT)
    small = pltpu.CompilerParams(vmem_limit_bytes=VMEM_LIMIT // 4)

    def facing(value, turn):
        return lax.ppermute(value, "leaf", [(i, i ^ turn) for i in range(leaf_total)])

    def beside(value):
        other = [min(max(((i + 1) ^ 1) - 1, 0), leaf_total - 1) for i in range(leaf_total)]
        return lax.ppermute(value, "leaf", list(enumerate(other)))

    def crossed(value, step):
        return lax.ppermute(value, "rep", [(i, i ^ step) for i in range(reps)])

    def members(value):
        found = [value]
        for k in range(1, reps):
            found.append(crossed(found[k - 1], 1) if k % 2 else crossed(value, k))
        return found

    near_count = near_lists.shape[1]
    raw_lists = (near_lists.T, couple_leaf.T, couple_pair.T, couple_quad)

    capacity = max(8, 2 * leaves // leaf_total)
    sent = pl.pallas_call(
        functools.partial(send_kernel, leaf_total, (leaves * reps).bit_length() - 1),
        out_shape=(jax.ShapeDtypeStruct((leaf_total * capacity, leaves), f32),)
        + (jax.ShapeDtypeStruct((capacity, 2 * LANES), f32),) * leaf_total,
        in_specs=[vmem, vmem],
        out_specs=(vmem,) * (leaf_total + 1),
        compiler_params=params,
        name="send",
    )(leaf_order.reshape(1, leaves), start_residual)
    slots, ordered = sent[0], [sent[1]] + [facing(sent[k + 1], k) for k in range(1, leaf_total)]
    up = (leaf_basis, transfer_one, transfer_two)
    matrices = up + (coupling_leaf, coupling_pair, coupling_quad)
    room = lambda arrays: [pltpu.SemaphoreType.DMA((len(arrays),))] + [pltpu.VMEM(m.shape, f32) for m in arrays]
    payload, own, mask, lists, arrive = pl.pallas_call(
        functools.partial(order_kernel, leaf_total, reps),
        out_shape=(jax.ShapeDtypeStruct((leaves, 4 * LANES), f32),)
        + (jax.ShapeDtypeStruct((leaves, width), f32),) * 2
        + (
            jax.ShapeDtypeStruct((32, leaves), jnp.int32),
            jax.ShapeDtypeStruct((leaf_total * capacity, leaves), f32),
        ),
        in_specs=[vmem] * (leaf_total + 7) + [hbm] * 3,
        out_specs=(vmem,) * 5,
        scratch_shapes=room(up)[1:] + room(up)[:1],
        compiler_params=params,
        name="order",
    )(*ordered, leaf_padding.reshape(1, leaves), point_coords, point_weights, *raw_lists, *up)
    gathered = members(jnp.concatenate([payload, facing(payload, 1), beside(payload)], axis=0))
    scratch = room(matrices) + [pltpu.VMEM((3 * leaves * reps, LANES), f32)] * 8
    scratch = scratch + [pltpu.VMEM((leaves, width, LANES), f32), pltpu.VMEM((width, LANES), f32)]
    scratch = scratch + [pltpu.VMEM((rank, LANES), f32)] * 3
    first = pl.pallas_call(
        functools.partial(first_kernel, reps, near_count),
        out_shape=jax.ShapeDtypeStruct((leaves, 2 * LANES), f32),
        in_specs=[smem] + [vmem] * (reps + 3) + [hbm] * 6,
        out_specs=vmem,
        scratch_shapes=scratch,
        compiler_params=params,
        name="first",
    )(lists, *gathered, own, mask, point_coords, *matrices)
    later = members(jnp.concatenate([first, facing(first, 1), beside(first)], axis=0))
    second = pl.pallas_call(
        functools.partial(second_kernel, reps, near_count),
        out_shape=(jax.ShapeDtypeStruct((capacity, 4 * LANES), f32),) * leaf_total,
        in_specs=[smem] + [vmem] * (2 * reps + 5) + [hbm] * 6,
        out_specs=(vmem,) * leaf_total,
        scratch_shapes=scratch,
        compiler_params=params,
        name="second",
    )(lists, *gathered, *later, own, first, mask, point_coords, arrive, *matrices)
    seconds = [second[0]] + [facing(second[k], k) for k in range(1, leaf_total)]
    last = sum(shard[:8, 2 * width :] for shard in seconds)
    lasts = [last] + [crossed(last, k) for k in range(1, reps)]
    second_image, first_image = pl.pallas_call(
        pick_kernel,
        out_shape=(jax.ShapeDtypeStruct((leaves, width), f32),) * 2,
        in_specs=[vmem] * (1 + leaf_total),
        out_specs=(vmem, vmem),
        compiler_params=small,
        name="pick",
    )(slots, *seconds)
    return pl.pallas_call(
        finish_kernel,
        out_shape=(jax.ShapeDtypeStruct((leaves, width), f32),) * 2,
        in_specs=[vmem] * (4 + reps),
        out_specs=(vmem, vmem),
        compiler_params=small,
        name="finish",
    )(start_point, start_residual, first_image, second_image, *lasts)


def solution(mesh):
    line = P(("groups", "leaf", "rep"))
    two = P(("groups", "leaf", "rep"), None)
    three = P(("groups", "leaf", "rep"), None, None)
    four = P(("groups", "leaf", "rep"), None, None, None)
    placed = (two, two, line, line, two, two, three, three, three, two, two, two, four, four, four, two)
    return jax.shard_map(body, mesh=mesh, in_specs=placed, out_specs=(two, two), check_vma=False)
```

```python
import functools

import jax
import jax.numpy as jnp
from jax import lax
from jax.experimental import pallas as pl
from jax.experimental.pallas import tpu as pltpu
from jax.sharding import PartitionSpec as P

PRECISE = lax.Precision.HIGHEST
JUMP = 0.5
SMOOTH_SQUARE = 0.01
KELVIN_DIAG = 2.2
EPSILON = 1e-06
LANES = 128
VMEM_LIMIT = 60 * 1024 * 1024


def lane_ids(rows):
    return lax.broadcasted_iota(jnp.int32, (rows, LANES), 1)


def columns_of(rows, count, column):
    lanes = lane_ids(rows)
    table = jnp.zeros((rows, LANES), jnp.float32)
    for g in range(count):
        table = jnp.where(lanes == g, column(g), table)
    return table


def lane_sum(value):
    return jnp.sum(value, axis=1, keepdims=True)


def expansions(masked, basis_ref, one_ref, two_ref):
    leaves, rank = basis_ref.shape[0], basis_ref.shape[1]
    leaf_columns = columns_of(rank, leaves, lambda g: lane_sum(basis_ref[g] * masked[g : g + 1, :]))
    leaf_rows = leaf_columns.T[:leaves, :]
    pair_columns = columns_of(
        rank,
        leaves // 2,
        lambda c: lane_sum(
            one_ref[2 * c] * leaf_rows[2 * c : 2 * c + 1, :]
            + one_ref[2 * c + 1] * leaf_rows[2 * c + 1 : 2 * c + 2, :]
        ),
    )
    pair_rows = pair_columns.T[: leaves // 2, :]
    quad_columns = columns_of(
        rank,
        leaves // 4,
        lambda c: lane_sum(
            two_ref[2 * c] * pair_rows[2 * c : 2 * c + 1, :]
            + two_ref[2 * c + 1] * pair_rows[2 * c + 1 : 2 * c + 2, :]
        ),
    )
    quad_rows = quad_columns.T[: leaves // 4, :]
    rest = jnp.zeros((leaves - leaves // 2 - leaves // 4, rank), jnp.float32)
    upper = jnp.concatenate([pair_rows, quad_rows, rest], axis=0)
    return jnp.concatenate([leaf_rows, upper], axis=1)


def start_copies(sources, targets, sems):
    copies = [pltpu.make_async_copy(x, y, sems.at[i]) for i, (x, y) in enumerate(zip(sources, targets))]
    for copy in copies:
        copy.start()
    return copies


def exact_dot(left, right, dims=((1,), (0,))):
    return lax.dot_general(left, right, (dims, ((), ())), precision=PRECISE, preferred_element_type=jnp.float32)


def send_kernel(leaf_total, bits, order_ref, residual_ref, slots_ref, *outs):
    leaves, width = residual_ref.shape
    capacity = outs[0].shape[0]
    order = order_ref[...]
    turned = (order >> bits) ^ lax.axis_index("leaf")
    ids = lax.broadcasted_iota(jnp.int32, (8 * ((leaf_total + 7) // 8), leaves), 0)
    mine = (turned == ids).astype(jnp.float32)
    row, column = [lax.broadcasted_iota(jnp.int32, (leaves, leaves), i) for i in (0, 1)]
    rank = exact_dot(mine, (row < column).astype(jnp.float32))
    slot = lax.broadcasted_iota(jnp.int32, (capacity, leaves), 0).astype(jnp.float32)
    position = ((order & (leaves - 1)) + 1).astype(jnp.float32)
    slots = jnp.concatenate(
        [jnp.where(slot == rank[k : k + 1, :], mine[k : k + 1, :], 0.0) for k in range(leaf_total)], axis=0
    )
    slots_ref[...] = slots
    rows = exact_dot(slots, residual_ref[...])
    place = jnp.broadcast_to(lane_sum(slots * position), (leaf_total * capacity, 2 * LANES - width))
    payload = jnp.concatenate([rows, place], axis=1)
    for k in range(leaf_total):
        outs[k][...] = payload[k * capacity : (k + 1) * capacity, :]


def order_kernel(leaf_total, reps, *refs):
    shards = refs[:leaf_total]
    padding_ref, coords_ref, weight_ref, *raw_lists = refs[leaf_total : leaf_total + 7]
    sources, (out_ref, vector_ref, mask_ref, lists_ref, arrive_ref) = refs[leaf_total + 7 : -9], refs[-9:-4]
    basis_ref, one_ref, two_ref, sems = refs[-4:]
    copies = start_copies(sources, (basis_ref, one_ref, two_ref), sems)
    leaves, width = vector_ref.shape
    leaf_index, rep_index = lax.axis_index("leaf"), lax.axis_index("rep")
    lists_ref[...] = jnp.zeros_like(lists_ref)
    for i, raw in enumerate(raw_lists):
        entries = raw[...]
        height = max(i - 1, 0)
        bits = (leaves >> height).bit_length() - 1
        owner = entries >> bits
        turned = (owner >> (reps.bit_length() - 1)) ^ leaf_index
        member = (owner & (reps - 1)) ^ rep_index
        side = (member & 1) * 3 + jnp.where(turned > 1, 2, turned)
        place = side * (reps // 2) + (member >> 1)
        row = place * leaves + (entries & ((1 << bits) - 1)) + (leaves // 2 if i == 3 else 0)
        lists_ref[8 * i : 8 * i + row.shape[0], 0 : row.shape[1]] = row
    points = weight_ref.shape[1]
    rows = jnp.concatenate([shard[...] for shard in shards], axis=0)
    ids = lax.broadcasted_iota(jnp.int32, (rows.shape[0], leaves), 1) + 1
    arrive = (rows[:, width : width + 1] == ids.astype(jnp.float32)).astype(jnp.float32)
    arrive_ref[...] = arrive
    vector = exact_dot(arrive, rows, ((0,), (0,)))[:, :width]
    row, column = [lax.broadcasted_iota(jnp.int32, (leaves, leaves), i) for i in (0, 1)]
    padding = lane_sum(jnp.where(row == column, padding_ref[...].astype(jnp.float32), 0.0))
    point = lax.broadcasted_iota(jnp.int32, (leaves, width), 1) & (points - 1)
    mask = (point.astype(jnp.float32) < points - padding).astype(jnp.float32)
    mask_ref[...] = mask
    vector_ref[...] = vector
    for copy in copies:
        copy.wait()
    spread = expansions(mask * vector, basis_ref, one_ref, two_ref)
    weight = weight_ref[...] * mask[:, :points]
    out_ref[...] = jnp.concatenate([vector, spread, coords_ref[...], weight], axis=1)


def build_tables(place, geometry, vector, tables):
    rows = pl.ds(place * geometry.shape[0], geometry.shape[0])
    x_ref, y_ref, z_ref, u0_ref, u1_ref, u2_ref, leaf_ref, upper_ref = [ref.at[rows, :] for ref in tables]
    low = lane_ids(geometry.shape[0]) < 64
    swap = lambda v: pltpu.roll(v, 64, 1)
    first, second = geometry[:, :LANES], geometry[:, LANES:]
    first_swap, second_swap = swap(first), swap(second)
    x_ref[...] = jnp.where(low, first, first_swap)
    y_ref[...] = jnp.where(low, first_swap, first)
    z_ref[...] = jnp.where(low, second, second_swap)
    weight = jnp.where(low, second_swap, second)
    head, tail = vector[:, :LANES], vector[:, LANES:]
    head_swap, tail_swap = swap(head), swap(tail)
    u0_ref[...] = jnp.where(low, head, head_swap) * weight
    u1_ref[...] = jnp.where(low, head_swap, head) * weight
    u2_ref[...] = jnp.where(low, tail, tail_swap) * weight
    leaf_ref[...] = tail_swap
    upper_ref[...] = pltpu.roll(tail, 32, 1)


def near_field(lists_ref, near_count, target_ref, tables, out_ref):
    leaves, points = target_ref.shape[0], target_ref.shape[1] // 3
    low = lane_ids(8) < 64
    lanes = lane_ids(8)
    out_ref[...] = jnp.zeros_like(out_ref)

    def leaf_field(g):
        sources = []
        for k in range(0, near_count, 2):
            one, other = lists_ref[k, g], lists_ref[k + 1, g]
            values = [
                jnp.where(
                    low,
                    jnp.broadcast_to(ref[pl.ds(one, 1), :], (8, LANES)),
                    jnp.broadcast_to(ref[pl.ds(other, 1), :], (8, LANES)),
                )
                for ref in tables[:6]
            ]
            sources.append(values)
        for p in range(0, points, 8):
            tx, ty, tz = [target_ref[g, a * points + p : a * points + p + 8, :] for a in range(3)]
            direct = bent = None
            for x, y, z, u0, u1, u2 in sources:
                dx, dy, dz = tx - x, ty - y, tz - z
                inverse = lax.rsqrt(dx * dx + dy * dy + (dz * dz + SMOOTH_SQUARE))
                along = dx * u0 + dy * u1 + dz * u2
                cubic = (inverse * inverse) * (inverse * along)
                terms = [inverse * u0, inverse * u1, inverse * u2], [cubic * dx, cubic * dy, cubic * dz]
                direct = terms[0] if direct is None else [s + t for s, t in zip(direct, terms[0])]
                bent = terms[1] if bent is None else [s + t for s, t in zip(bent, terms[1])]
            sums = [KELVIN_DIAG * s + t for s, t in zip(direct, bent)]
            for a in range(3):
                rows = pl.ds(a * points + p, 8)
                out_ref[rows, :] = jnp.where(lanes == g, lane_sum(sums[a]), out_ref[rows, :])

    def some_leaves(step, carry):
        for u in range(8):
            leaf_field(step * 8 + u)
        return carry

    lax.fori_loop(0, leaves // 8, some_leaves, 0)


def coupled(entry, matrix_ref, table_ref, field_ref):
    count, partners, rank = matrix_ref.shape[:3]
    lanes = lane_ids(rank)
    step = 8

    def cluster_step(s, field):
        for u in range(step):
            t = s * step + u
            total = None
            for k in range(partners):
                row = table_ref[pl.ds(entry(t, k), 1), :][:, :rank]
                term = matrix_ref[t, k] * row
                total = term if total is None else total + term
            field = jnp.where(lanes == t, lane_sum(total), field)
        return field

    field_ref[...] = lax.fori_loop(0, count // step, cluster_step, jnp.zeros((rank, LANES), jnp.float32))


def rows_of(columns, matrix_ref, share):
    count = matrix_ref.shape[0]
    rows = []
    for c in range(count):
        column = columns[:, c // share : c // share + 1]
        rows.append(jnp.sum(matrix_ref[c] * column, axis=0, keepdims=True))
    return jnp.concatenate(rows, axis=0)


def columns_from_rows(rows):
    count, width = rows.shape
    padded = jnp.concatenate([rows, jnp.zeros((count, LANES - width), jnp.float32)], axis=1)
    full = jnp.concatenate([padded, jnp.zeros((LANES - count, LANES), jnp.float32)], axis=0)
    return full.T[:width, :]


def fill_targets(coords, target_ref):
    leaves, width = coords.shape
    padded = jnp.concatenate([coords, jnp.zeros((LANES - leaves, width), jnp.float32)], axis=0)
    columns = padded.T
    for g in range(leaves):
        target_ref[g] = jnp.broadcast_to(columns[:, g : g + 1], (width, LANES))


def operator(own, mask, lists_ref, near_count, copies, held, tables, scratch):
    basis_ref, one_ref, two_ref, c_leaf, c_pair, c_quad = held
    target_ref, near_out, f_leaf, f_pair, f_quad = scratch
    leaves = own.shape[0]
    near_field(lists_ref, near_count, target_ref, tables, near_out)
    for copy in copies:
        copy.wait()
    coupled(lambda t, k: lists_ref[24 + t, k], c_quad, tables[7], f_quad)
    coupled(lambda t, k: lists_ref[16 + k, t], c_pair, tables[7], f_pair)
    coupled(lambda t, k: lists_ref[8 + k, t], c_leaf, tables[6], f_leaf)
    total_pair = f_pair[...] + columns_from_rows(rows_of(f_quad[...], two_ref, 2))
    total_leaf = f_leaf[...] + columns_from_rows(rows_of(total_pair, one_ref, 2))
    far = rows_of(total_leaf, basis_ref, 1)
    near = near_out[...].T[:leaves, :]
    return mask * (JUMP * (mask * own) + near + far) + (1.0 - mask) * own


def total_of(value):
    return jnp.sum(jnp.sum(value, axis=1, keepdims=True), axis=0, keepdims=True)


def in_lanes(values):
    lanes = lane_ids(8)
    table = jnp.zeros((8, LANES), jnp.float32)
    for g, value in enumerate(values):
        table = jnp.where(lanes == g, value, table)
    return table


def first_kernel(parts, near_count, lists_ref, *refs):
    gathered, (own_ref, mask_ref, coords_ref), sources = refs[:parts], refs[parts : parts + 3], refs[parts + 3 : parts + 9]
    out_ref, sems = refs[parts + 9 : parts + 11]
    held, tables, scratch = refs[parts + 11 : parts + 17], refs[parts + 17 : parts + 25], refs[parts + 25 :]
    copies = start_copies(sources, held, sems)
    fill_targets(coords_ref[...], scratch[0])
    for i in range(parts):
        build_tables(i, gathered[i][:, 256:], gathered[i][:, :256], tables)
    own, mask = own_ref[...], mask_ref[...]
    image = operator(own, mask, lists_ref, near_count, copies, held, tables, scratch)
    spread = expansions(mask * image, *held[:3])
    out_ref[...] = jnp.concatenate([image, spread], axis=1)


def second_kernel(parts, near_count, lists_ref, *refs):
    gathered, later, refs = refs[:parts], refs[parts : 2 * parts], refs[2 * parts :]
    residual_ref, own_ref, mask_ref, coords_ref, arrive_ref = refs[:5]
    sources, outs, sems = refs[5:11], refs[11:-20], refs[-20]
    held, tables, scratch = refs[-19:-13], refs[-13:-5], refs[-5:]
    copies = start_copies(sources, held, sems)
    fill_targets(coords_ref[...], scratch[0])
    for i in range(parts):
        build_tables(i, gathered[i][:, 256:], later[i][...], tables)
    residual, mask = residual_ref[...], mask_ref[...]
    width = residual.shape[1]
    own = own_ref[:, :width]
    image = operator(own, mask, lists_ref, near_count, copies, held, tables, scratch)
    pairs = ((residual, residual), (residual, own), (own, own), (residual, image), (own, image), (image, image))
    sums = in_lanes([total_of(x * y) for x, y in pairs])
    capacity = outs[0].shape[0]
    if capacity > 8:
        sums = jnp.concatenate([sums, jnp.zeros((capacity - 8, LANES), jnp.float32)], axis=0)
    rows = exact_dot(arrive_ref[...], jnp.concatenate([image, own], axis=1))
    for k, out_ref in enumerate(outs):
        out_ref[...] = jnp.concatenate([rows[k * capacity : (k + 1) * capacity, :], sums], axis=1)


def pick_kernel(slots_ref, *refs):
    shards, (second_ref, first_ref) = refs[:-2], refs[-2:]
    width = first_ref.shape[1]
    rows = jnp.concatenate([shard[...] for shard in shards], axis=0)
    found = exact_dot(slots_ref[...], rows[:, : 2 * width], ((0,), (0,)))
    second_ref[...] = found[:, :width]
    first_ref[...] = found[:, width:]


def finish_kernel(point_ref, residual_ref, first_ref, second_ref, *refs):
    next_point, next_residual = refs[-2:]
    sums = sum(ref[...] for ref in refs[:-2])
    rr, rw, ww, rv, wv, vv = [sums[0:1, j : j + 1] for j in range(6)]
    scale_square = rr + EPSILON
    scale = jnp.sqrt(scale_square)
    norm = rr / scale_square
    top_first = rw / scale_square
    rest_square = (ww - 2.0 * top_first * rw + top_first * top_first * rr) / scale_square
    along_image = (rv - top_first * rw) / scale_square
    rest_image = (wv - top_first * ww - top_first * (rv - top_first * rw)) / scale_square
    image_square = (vv - 2.0 * top_first * wv + top_first * top_first * ww) / scale_square
    rest_square = jnp.maximum(rest_square, 0.0)
    below_square = rest_square + EPSILON
    below_first = jnp.sqrt(below_square)
    top_second = along_image / below_first
    mid_second = rest_image / below_square
    image_square = image_square / below_square
    one_square = rest_square / below_square
    cross = (top_first - top_first * norm) / below_first
    below_second_square = (
        image_square
        - 2.0 * top_second * top_second
        - 2.0 * mid_second * mid_second
        + top_second * top_second * norm
        + mid_second * mid_second * one_square
        + 2.0 * top_second * mid_second * cross
        + EPSILON
    )
    gram_first = top_first * top_first + below_square
    gram_cross = top_first * top_second + below_first * mid_second
    gram_second = top_second * top_second + mid_second * mid_second + below_second_square
    determinant = gram_first * gram_second - gram_cross * gram_cross
    step_zero = scale * (gram_second * top_first - gram_cross * top_second) / determinant
    step_one = scale * (gram_first * top_second - gram_cross * top_first) / determinant
    residual, first = residual_ref[...], first_ref[...]
    rest = first - top_first * residual
    rest_image = second_ref[...] - top_first * first
    along_zero = step_zero / scale
    along_one = step_one / (scale * below_first)
    next_point[...] = point_ref[...] + along_zero * residual + along_one * rest
    next_residual[...] = residual - along_zero * first - along_one * rest_image


def body(
    start_point,
    start_residual,
    leaf_order,
    leaf_padding,
    point_coords,
    point_weights,
    leaf_basis,
    transfer_one,
    transfer_two,
    couple_leaf,
    couple_pair,
    couple_quad,
    coupling_leaf,
    coupling_pair,
    coupling_quad,
    near_lists,
):
    leaves, width = start_point.shape
    points = point_weights.shape[1]
    rank = leaf_basis.shape[1]
    leaf_total = lax.axis_size("leaf")
    reps = lax.axis_size("rep")
    f32 = jnp.float32
    vmem = pl.BlockSpec(memory_space=pltpu.VMEM)
    smem = pl.BlockSpec(memory_space=pltpu.SMEM)
    hbm = pl.BlockSpec(memory_space=pltpu.HBM)
    params = pltpu.CompilerParams(vmem_limit_bytes=VMEM_LIMIT)
    small = pltpu.CompilerParams(vmem_limit_bytes=VMEM_LIMIT // 4)

    def facing(value, turn):
        return lax.ppermute(value, "leaf", [(i, i ^ turn) for i in range(leaf_total)])

    def beside(value):
        other = [min(max(((i + 1) ^ 1) - 1, 0), leaf_total - 1) for i in range(leaf_total)]
        return lax.ppermute(value, "leaf", list(enumerate(other)))

    def crossed(value, step):
        return lax.ppermute(value, "rep", [(i, i ^ step) for i in range(reps)])

    def nearby(value):
        found = []
        others = [min(max(((i + 1) ^ 1) - 1, 0), leaf_total - 1) for i in range(leaf_total)]
        for along in (list(range(leaf_total)), [i ^ 1 for i in range(leaf_total)], others):
            for turn in range(0, reps, 2):
                pairs = [(i * reps + j, along[i] * reps + (j ^ turn)) for i in range(leaf_total) for j in range(reps)]
                moved = any(i != j for i, j in pairs)
                found.append(lax.ppermute(value, ("leaf", "rep"), pairs) if moved else value)
        return found + [crossed(part, 1) for part in found]

    near_count = near_lists.shape[1]
    raw_lists = (near_lists.T, couple_leaf.T, couple_pair.T, couple_quad)

    capacity = max(8, 2 * leaves // leaf_total)
    sent = pl.pallas_call(
        functools.partial(send_kernel, leaf_total, (leaves * reps).bit_length() - 1),
        out_shape=(jax.ShapeDtypeStruct((leaf_total * capacity, leaves), f32),)
        + (jax.ShapeDtypeStruct((capacity, 2 * LANES), f32),) * leaf_total,
        in_specs=[vmem, vmem],
        out_specs=(vmem,) * (leaf_total + 1),
        compiler_params=params,
        name="send",
    )(leaf_order.reshape(1, leaves), start_residual)
    slots, ordered = sent[0], [sent[1]] + [facing(sent[k + 1], k) for k in range(1, leaf_total)]
    up = (leaf_basis, transfer_one, transfer_two)
    matrices = up + (coupling_leaf, coupling_pair, coupling_quad)
    room = lambda arrays: [pltpu.SemaphoreType.DMA((len(arrays),))] + [pltpu.VMEM(m.shape, f32) for m in arrays]
    payload, own, mask, lists, arrive = pl.pallas_call(
        functools.partial(order_kernel, leaf_total, reps),
        out_shape=(jax.ShapeDtypeStruct((leaves, 4 * LANES), f32),)
        + (jax.ShapeDtypeStruct((leaves, width), f32),) * 2
        + (
            jax.ShapeDtypeStruct((32, leaves), jnp.int32),
            jax.ShapeDtypeStruct((leaf_total * capacity, leaves), f32),
        ),
        in_specs=[vmem] * (leaf_total + 7) + [hbm] * 3,
        out_specs=(vmem,) * 5,
        scratch_shapes=room(up)[1:] + room(up)[:1],
        compiler_params=params,
        name="order",
    )(*ordered, leaf_padding.reshape(1, leaves), point_coords, point_weights, *raw_lists, *up)
    gathered = nearby(payload)
    scratch = room(matrices) + [pltpu.VMEM((3 * leaves * reps, LANES), f32)] * 8
    scratch = scratch + [pltpu.VMEM((leaves, width, LANES), f32), pltpu.VMEM((width, LANES), f32)]
    scratch = scratch + [pltpu.VMEM((rank, LANES), f32)] * 3
    first = pl.pallas_call(
        functools.partial(first_kernel, len(gathered), near_count),
        out_shape=jax.ShapeDtypeStruct((leaves, 2 * LANES), f32),
        in_specs=[smem] + [vmem] * (len(gathered) + 3) + [hbm] * 6,
        out_specs=vmem,
        scratch_shapes=scratch,
        compiler_params=params,
        name="first",
    )(lists, *gathered, own, mask, point_coords, *matrices)
    later = nearby(first)
    second = pl.pallas_call(
        functools.partial(second_kernel, len(gathered), near_count),
        out_shape=(jax.ShapeDtypeStruct((capacity, 4 * LANES), f32),) * leaf_total,
        in_specs=[smem] + [vmem] * (2 * len(gathered) + 5) + [hbm] * 6,
        out_specs=(vmem,) * leaf_total,
        scratch_shapes=scratch,
        compiler_params=params,
        name="second",
    )(lists, *gathered, *later, own, first, mask, point_coords, arrive, *matrices)
    seconds = [second[0]] + [facing(second[k], k) for k in range(1, leaf_total)]
    last = sum(shard[:8, 2 * width :] for shard in seconds)
    lasts = [last] + [crossed(last, k) for k in range(1, reps)]
    second_image, first_image = pl.pallas_call(
        pick_kernel,
        out_shape=(jax.ShapeDtypeStruct((leaves, width), f32),) * 2,
        in_specs=[vmem] * (1 + leaf_total),
        out_specs=(vmem, vmem),
        compiler_params=small,
        name="pick",
    )(slots, *seconds)
    return pl.pallas_call(
        finish_kernel,
        out_shape=(jax.ShapeDtypeStruct((leaves, width), f32),) * 2,
        in_specs=[vmem] * (4 + reps),
        out_specs=(vmem, vmem),
        compiler_params=small,
        name="finish",
    )(start_point, start_residual, first_image, second_image, *lasts)


def solution(mesh):
    line = P(("groups", "leaf", "rep"))
    two = P(("groups", "leaf", "rep"), None)
    three = P(("groups", "leaf", "rep"), None, None)
    four = P(("groups", "leaf", "rep"), None, None, None)
    placed = (two, two, line, line, two, two, three, three, three, two, two, two, four, four, four, two)
    return jax.shard_map(body, mesh=mesh, in_specs=placed, out_specs=(two, two), check_vma=False)
```

```python
import functools

import jax
import jax.numpy as jnp
from jax import lax
from jax.experimental import pallas as pl
from jax.experimental.pallas import tpu as pltpu
from jax.sharding import PartitionSpec as P

PRECISE = lax.Precision.HIGHEST
JUMP = 0.5
SMOOTH_SQUARE = 0.01
KELVIN_DIAG = 2.2
EPSILON = 1e-06
LANES = 128
VMEM_LIMIT = 60 * 1024 * 1024


def lane_ids(rows):
    return lax.broadcasted_iota(jnp.int32, (rows, LANES), 1)


def columns_of(rows, count, column):
    lanes = lane_ids(rows)
    table = jnp.zeros((rows, LANES), jnp.float32)
    for g in range(count):
        table = jnp.where(lanes == g, column(g), table)
    return table


def lane_sum(value):
    return jnp.sum(value, axis=1, keepdims=True)


def expansions(masked, basis_ref, one_ref, two_ref, spare=None):
    leaves, rank = basis_ref.shape[0], basis_ref.shape[1]
    leaf_columns = columns_of(rank, leaves, lambda g: lane_sum(basis_ref[g] * masked[g : g + 1, :]))
    leaf_rows = leaf_columns.T[:leaves, :]
    pair_columns = columns_of(
        rank,
        leaves // 2,
        lambda c: lane_sum(
            one_ref[2 * c] * leaf_rows[2 * c : 2 * c + 1, :]
            + one_ref[2 * c + 1] * leaf_rows[2 * c + 1 : 2 * c + 2, :]
        ),
    )
    pair_rows = pair_columns.T[: leaves // 2, :]
    quad_columns = columns_of(
        rank,
        leaves // 4,
        lambda c: lane_sum(
            two_ref[2 * c] * pair_rows[2 * c : 2 * c + 1, :]
            + two_ref[2 * c + 1] * pair_rows[2 * c + 1 : 2 * c + 2, :]
        ),
    )
    quad_rows = quad_columns.T[: leaves // 4, :]
    if spare is None:
        spare = jnp.zeros((leaves - leaves // 2 - leaves // 4, rank), jnp.float32)
    upper = jnp.concatenate([pair_rows, quad_rows, spare], axis=0)
    return jnp.concatenate([leaf_rows, upper], axis=1)


def start_copies(sources, targets, sems):
    copies = [pltpu.make_async_copy(x, y, sems.at[i]) for i, (x, y) in enumerate(zip(sources, targets))]
    for copy in copies:
        copy.start()
    return copies


def exact_dot(left, right, dims=((1,), (0,))):
    return lax.dot_general(left, right, (dims, ((), ())), precision=PRECISE, preferred_element_type=jnp.float32)


def send_kernel(leaf_total, reps, order_ref, padding_ref, residual_ref, coords_ref, weight_ref, *refs):
    raw_lists, (slots_ref, side_ref, lists_ref), outs = refs[:4], refs[4:7], refs[7:]
    leaves, width = residual_ref.shape
    points = weight_ref.shape[1]
    leaf_index, rep_index = lax.axis_index("leaf"), lax.axis_index("rep")
    lists_ref[...] = jnp.zeros_like(lists_ref)
    for i, raw in enumerate(raw_lists):
        entries = raw[...]
        height = max(i - 1, 0)
        bits = (leaves >> height).bit_length() - 1
        owner = entries >> bits
        turned = (owner >> (reps.bit_length() - 1)) ^ leaf_index
        member = (owner & (reps - 1)) ^ rep_index
        side = (member & 1) * 3 + jnp.where(turned > 1, 2, turned)
        place = side * (reps // 2) + (member >> 1)
        row = place * leaves + (entries & ((1 << bits) - 1)) + (leaves // 2 if i == 3 else 0)
        lists_ref[8 * i : 8 * i + row.shape[0], 0 : row.shape[1]] = row
    capacity = outs[0].shape[0]
    order = order_ref[...]
    turned = (order >> ((leaves * reps).bit_length() - 1)) ^ leaf_index
    ids = lax.broadcasted_iota(jnp.int32, (8 * ((leaf_total + 7) // 8), leaves), 0)
    mine = (turned == ids).astype(jnp.float32)
    row, column = [lax.broadcasted_iota(jnp.int32, (leaves, leaves), i) for i in (0, 1)]
    padding = lane_sum(jnp.where(row == column, padding_ref[...].astype(jnp.float32), 0.0))
    point = lax.broadcasted_iota(jnp.int32, (leaves, width), 1) & (points - 1)
    mask = (point.astype(jnp.float32) < points - padding).astype(jnp.float32)
    weight = weight_ref[...] * mask[:, :points]
    side_ref[...] = jnp.concatenate([coords_ref[...], weight, mask, jnp.zeros((leaves, points), jnp.float32)], axis=1)
    rank = exact_dot(mine, (row < column).astype(jnp.float32))
    slot = lax.broadcasted_iota(jnp.int32, (capacity, leaves), 0).astype(jnp.float32)
    position = ((order & (leaves - 1)) + 1).astype(jnp.float32)
    slots = jnp.concatenate(
        [jnp.where(slot == rank[k : k + 1, :], mine[k : k + 1, :], 0.0) for k in range(leaf_total)], axis=0
    )
    slots_ref[...] = slots
    rows = exact_dot(slots, residual_ref[...])
    place = jnp.broadcast_to(lane_sum(slots * position), (leaf_total * capacity, 2 * LANES - width))
    payload = jnp.concatenate([rows, place], axis=1)
    for k in range(leaf_total):
        outs[k][...] = payload[k * capacity : (k + 1) * capacity, :]


def fetch_kernel(*refs):
    count = len(refs) // 2
    for copy in start_copies(refs[:count], refs[count:-1], refs[-1]):
        copy.wait()


def order_kernel(leaf_total, width, *refs):
    shards = refs[:leaf_total]
    side_ref, basis_ref, one_ref, two_ref, out_ref = refs[leaf_total:]
    leaves = side_ref.shape[0]
    rows = jnp.concatenate([shard[...] for shard in shards], axis=0)
    ids = lax.broadcasted_iota(jnp.int32, (rows.shape[0], leaves), 1) + 1
    arrive = (rows[:, width : width + 1] == ids.astype(jnp.float32)).astype(jnp.float32)
    places = exact_dot(ids[:8, :].astype(jnp.float32), arrive, ((1,), (1,)))[:1, :]
    spare = [places[:, i : i + leaves] for i in range(0, arrive.shape[0], leaves)]
    spare = jnp.concatenate(spare + [jnp.zeros((8 - len(spare), leaves), jnp.float32)], axis=0)
    vector = exact_dot(arrive, rows, ((0,), (0,)))[:, :width]
    spread = expansions(side_ref[:, 256 : 256 + width] * vector, basis_ref, one_ref, two_ref, spare)
    out_ref[...] = jnp.concatenate([vector, spread, side_ref[:, :256]], axis=1)


def build_tables(place, geometry, vector, tables):
    rows = pl.ds(place * geometry.shape[0], geometry.shape[0])
    x_ref, y_ref, z_ref, u0_ref, u1_ref, u2_ref, leaf_ref, upper_ref = [ref.at[rows, :] for ref in tables]
    low = lane_ids(geometry.shape[0]) < 64
    swap = lambda v: pltpu.roll(v, 64, 1)
    first, second = geometry[:, :LANES], geometry[:, LANES:]
    first_swap, second_swap = swap(first), swap(second)
    x_ref[...] = jnp.where(low, first, first_swap)
    y_ref[...] = jnp.where(low, first_swap, first)
    z_ref[...] = jnp.where(low, second, second_swap)
    weight = jnp.where(low, second_swap, second)
    head, tail = vector[:, :LANES], vector[:, LANES:]
    head_swap, tail_swap = swap(head), swap(tail)
    u0_ref[...] = jnp.where(low, head, head_swap) * weight
    u1_ref[...] = jnp.where(low, head_swap, head) * weight
    u2_ref[...] = jnp.where(low, tail, tail_swap) * weight
    leaf_ref[...] = tail_swap
    upper_ref[...] = pltpu.roll(tail, 32, 1)


def near_field(lists_ref, near_count, target_ref, tables, out_ref):
    leaves, points = target_ref.shape[0], target_ref.shape[1] // 3
    low = lane_ids(8) < 64
    lanes = lane_ids(8)
    out_ref[...] = jnp.zeros_like(out_ref)

    def leaf_field(g):
        sources = []
        for k in range(0, near_count, 2):
            one, other = lists_ref[k, g], lists_ref[k + 1, g]
            values = [
                jnp.where(
                    low,
                    jnp.broadcast_to(ref[pl.ds(one, 1), :], (8, LANES)),
                    jnp.broadcast_to(ref[pl.ds(other, 1), :], (8, LANES)),
                )
                for ref in tables[:6]
            ]
            sources.append(values)
        for p in range(0, points, 8):
            tx, ty, tz = [target_ref[g, a * points + p : a * points + p + 8, :] for a in range(3)]
            direct = bent = None
            for x, y, z, u0, u1, u2 in sources:
                dx, dy, dz = tx - x, ty - y, tz - z
                inverse = lax.rsqrt(dx * dx + dy * dy + (dz * dz + SMOOTH_SQUARE))
                along = dx * u0 + dy * u1 + dz * u2
                cubic = (inverse * inverse) * (inverse * along)
                terms = [inverse * u0, inverse * u1, inverse * u2], [cubic * dx, cubic * dy, cubic * dz]
                direct = terms[0] if direct is None else [s + t for s, t in zip(direct, terms[0])]
                bent = terms[1] if bent is None else [s + t for s, t in zip(bent, terms[1])]
            sums = [KELVIN_DIAG * s + t for s, t in zip(direct, bent)]
            for a in range(3):
                rows = pl.ds(a * points + p, 8)
                out_ref[rows, :] = jnp.where(lanes == g, lane_sum(sums[a]), out_ref[rows, :])

    def some_leaves(step, carry):
        for u in range(8):
            leaf_field(step * 8 + u)
        return carry

    lax.fori_loop(0, leaves // 8, some_leaves, 0)


def coupled(entry, matrix_ref, table_ref, field_ref):
    count, partners, rank = matrix_ref.shape[:3]
    lanes = lane_ids(rank)
    step = 8

    def cluster_step(s, field):
        for u in range(step):
            t = s * step + u
            total = None
            for k in range(partners):
                row = table_ref[pl.ds(entry(t, k), 1), :][:, :rank]
                term = matrix_ref[t, k] * row
                total = term if total is None else total + term
            field = jnp.where(lanes == t, lane_sum(total), field)
        return field

    field_ref[...] = lax.fori_loop(0, count // step, cluster_step, jnp.zeros((rank, LANES), jnp.float32))


def rows_of(columns, matrix_ref, share):
    count = matrix_ref.shape[0]
    rows = []
    for c in range(count):
        column = columns[:, c // share : c // share + 1]
        rows.append(jnp.sum(matrix_ref[c] * column, axis=0, keepdims=True))
    return jnp.concatenate(rows, axis=0)


def columns_from_rows(rows):
    count, width = rows.shape
    padded = jnp.concatenate([rows, jnp.zeros((count, LANES - width), jnp.float32)], axis=1)
    full = jnp.concatenate([padded, jnp.zeros((LANES - count, LANES), jnp.float32)], axis=0)
    return full.T[:width, :]


def fill_targets(coords, target_ref):
    leaves, width = coords.shape
    padded = jnp.concatenate([coords, jnp.zeros((LANES - leaves, width), jnp.float32)], axis=0)
    columns = padded.T
    for g in range(leaves):
        target_ref[g] = jnp.broadcast_to(columns[:, g : g + 1], (width, LANES))


def operator(own, mask, lists_ref, near_count, copies, held, tables, scratch):
    basis_ref, one_ref, two_ref, c_leaf, c_pair, c_quad = held
    target_ref, near_out, f_leaf, f_pair, f_quad = scratch
    leaves = own.shape[0]
    near_field(lists_ref, near_count, target_ref, tables, near_out)
    for copy in copies:
        copy.wait()
    coupled(lambda t, k: lists_ref[24 + t, k], c_quad, tables[7], f_quad)
    coupled(lambda t, k: lists_ref[16 + k, t], c_pair, tables[7], f_pair)
    coupled(lambda t, k: lists_ref[8 + k, t], c_leaf, tables[6], f_leaf)
    total_pair = f_pair[...] + columns_from_rows(rows_of(f_quad[...], two_ref, 2))
    total_leaf = f_leaf[...] + columns_from_rows(rows_of(total_pair, one_ref, 2))
    far = rows_of(total_leaf, basis_ref, 1)
    near = near_out[...].T[:leaves, :]
    return mask * (JUMP * (mask * own) + near + far) + (1.0 - mask) * own


def total_of(value):
    return jnp.sum(jnp.sum(value, axis=1, keepdims=True), axis=0, keepdims=True)


def in_lanes(values):
    lanes = lane_ids(8)
    table = jnp.zeros((8, LANES), jnp.float32)
    for g, value in enumerate(values):
        table = jnp.where(lanes == g, value, table)
    return table


def first_kernel(parts, near_count, lists_ref, *refs):
    gathered, side_ref, sources = refs[:parts], refs[parts], refs[parts + 1 : parts + 7]
    out_ref, sems = refs[parts + 7 : parts + 9]
    held, tables, scratch = refs[parts + 9 : parts + 15], refs[parts + 15 : parts + 23], refs[parts + 23 :]
    width = held[0].shape[2]
    copies = start_copies(sources, held, sems)
    fill_targets(side_ref[:, :width], scratch[0])
    for i in range(parts):
        build_tables(i, gathered[i][:, 256:], gathered[i][:, :256], tables)
    own, mask = gathered[0][:, :width], side_ref[:, 256 : 256 + width]
    image = operator(own, mask, lists_ref, near_count, copies, held, tables, scratch)
    spread = expansions(mask * image, *held[:3])
    out_ref[...] = jnp.concatenate([image, spread], axis=1)


def second_kernel(parts, near_count, lists_ref, *refs):
    gathered, later, refs = refs[:parts], refs[parts : 2 * parts], refs[2 * parts :]
    side_ref, sources, outs, sems = refs[0], refs[1:7], refs[7:-20], refs[-20]
    held, tables, scratch = refs[-19:-13], refs[-13:-5], refs[-5:]
    width = held[0].shape[2]
    copies = start_copies(sources, held, sems)
    fill_targets(side_ref[:, :width], scratch[0])
    for i in range(parts):
        build_tables(i, gathered[i][:, 256:], later[i][...], tables)
    residual, own, mask = gathered[0][:, :width], later[0][:, :width], side_ref[:, 256 : 256 + width]
    image = operator(own, mask, lists_ref, near_count, copies, held, tables, scratch)
    pairs = ((residual, residual), (residual, own), (own, own), (residual, image), (own, image), (image, image))
    sums = in_lanes([total_of(x * y) for x, y in pairs])
    capacity = outs[0].shape[0]
    if capacity > 8:
        sums = jnp.concatenate([sums, jnp.zeros((capacity - 8, LANES), jnp.float32)], axis=0)
    leaves = own.shape[0]
    free = leaves // 2 + leaves // 4
    at = range(free, free + len(outs) * capacity // leaves)
    places = jnp.concatenate([gathered[0][i : i + 1, 2 * LANES - leaves : 2 * LANES] for i in at], axis=1)
    ids = lax.broadcasted_iota(jnp.int32, (leaves, places.shape[1]), 0) + 1
    arrive = (places == ids.astype(jnp.float32)).astype(jnp.float32)
    rows = exact_dot(arrive, jnp.concatenate([image, own], axis=1), ((0,), (0,)))
    for k, out_ref in enumerate(outs):
        out_ref[...] = jnp.concatenate([rows[k * capacity : (k + 1) * capacity, :], sums], axis=1)


def pick_kernel(slots_ref, *refs):
    shards, (second_ref, first_ref) = refs[:-2], refs[-2:]
    width = first_ref.shape[1]
    rows = jnp.concatenate([shard[...] for shard in shards], axis=0)
    found = exact_dot(slots_ref[...], rows[:, : 2 * width], ((0,), (0,)))
    second_ref[...] = found[:, :width]
    first_ref[...] = found[:, width:]


def finish_kernel(point_ref, residual_ref, first_ref, second_ref, *refs):
    next_point, next_residual = refs[-2:]
    sums = sum(ref[...] for ref in refs[:-2])
    rr, rw, ww, rv, wv, vv = [sums[0:1, j : j + 1] for j in range(6)]
    scale_square = rr + EPSILON
    scale = jnp.sqrt(scale_square)
    norm = rr / scale_square
    top_first = rw / scale_square
    rest_square = (ww - 2.0 * top_first * rw + top_first * top_first * rr) / scale_square
    along_image = (rv - top_first * rw) / scale_square
    rest_image = (wv - top_first * ww - top_first * (rv - top_first * rw)) / scale_square
    image_square = (vv - 2.0 * top_first * wv + top_first * top_first * ww) / scale_square
    rest_square = jnp.maximum(rest_square, 0.0)
    below_square = rest_square + EPSILON
    below_first = jnp.sqrt(below_square)
    top_second = along_image / below_first
    mid_second = rest_image / below_square
    image_square = image_square / below_square
    one_square = rest_square / below_square
    cross = (top_first - top_first * norm) / below_first
    below_second_square = (
        image_square
        - 2.0 * top_second * top_second
        - 2.0 * mid_second * mid_second
        + top_second * top_second * norm
        + mid_second * mid_second * one_square
        + 2.0 * top_second * mid_second * cross
        + EPSILON
    )
    gram_first = top_first * top_first + below_square
    gram_cross = top_first * top_second + below_first * mid_second
    gram_second = top_second * top_second + mid_second * mid_second + below_second_square
    determinant = gram_first * gram_second - gram_cross * gram_cross
    step_zero = scale * (gram_second * top_first - gram_cross * top_second) / determinant
    step_one = scale * (gram_first * top_second - gram_cross * top_first) / determinant
    residual, first = residual_ref[...], first_ref[...]
    rest = first - top_first * residual
    rest_image = second_ref[...] - top_first * first
    along_zero = step_zero / scale
    along_one = step_one / (scale * below_first)
    next_point[...] = point_ref[...] + along_zero * residual + along_one * rest
    next_residual[...] = residual - along_zero * first - along_one * rest_image


def body(
    start_point,
    start_residual,
    leaf_order,
    leaf_padding,
    point_coords,
    point_weights,
    leaf_basis,
    transfer_one,
    transfer_two,
    couple_leaf,
    couple_pair,
    couple_quad,
    coupling_leaf,
    coupling_pair,
    coupling_quad,
    near_lists,
):
    leaves, width = start_point.shape
    points = point_weights.shape[1]
    rank = leaf_basis.shape[1]
    leaf_total = lax.axis_size("leaf")
    reps = lax.axis_size("rep")
    f32 = jnp.float32
    vmem = pl.BlockSpec(memory_space=pltpu.VMEM)
    smem = pl.BlockSpec(memory_space=pltpu.SMEM)
    hbm = pl.BlockSpec(memory_space=pltpu.HBM)
    params = pltpu.CompilerParams(vmem_limit_bytes=VMEM_LIMIT)
    small = pltpu.CompilerParams(vmem_limit_bytes=VMEM_LIMIT // 4)

    def facing(value, turn):
        return lax.ppermute(value, "leaf", [(i, i ^ turn) for i in range(leaf_total)])

    def beside(value):
        other = [min(max(((i + 1) ^ 1) - 1, 0), leaf_total - 1) for i in range(leaf_total)]
        return lax.ppermute(value, "leaf", list(enumerate(other)))

    def crossed(value, step):
        return lax.ppermute(value, "rep", [(i, i ^ step) for i in range(reps)])

    def nearby(value):
        found = []
        others = [min(max(((i + 1) ^ 1) - 1, 0), leaf_total - 1) for i in range(leaf_total)]
        for along in (list(range(leaf_total)), [i ^ 1 for i in range(leaf_total)], others):
            for turn in range(0, reps, 2):
                pairs = [(i * reps + j, along[i] * reps + (j ^ turn)) for i in range(leaf_total) for j in range(reps)]
                moved = any(i != j for i, j in pairs)
                found.append(lax.ppermute(value, ("leaf", "rep"), pairs) if moved else value)
        return found + [crossed(part, 1) for part in found]

    near_count = near_lists.shape[1]
    raw_lists = (near_lists.T, couple_leaf.T, couple_pair.T, couple_quad)

    capacity = max(8, 2 * leaves // leaf_total)
    sent = pl.pallas_call(
        functools.partial(send_kernel, leaf_total, reps),
        out_shape=(
            jax.ShapeDtypeStruct((leaf_total * capacity, leaves), f32),
            jax.ShapeDtypeStruct((leaves, 4 * LANES), f32),
            jax.ShapeDtypeStruct((32, leaves), jnp.int32),
        )
        + (jax.ShapeDtypeStruct((capacity, 2 * LANES), f32),) * leaf_total,
        in_specs=[vmem] * 9,
        out_specs=(vmem,) * (leaf_total + 3),
        compiler_params=params,
        name="send",
    )(
        leaf_order.reshape(1, leaves),
        leaf_padding.reshape(1, leaves),
        start_residual,
        point_coords,
        point_weights,
        *raw_lists,
    )
    slots, side, lists, *sent = sent
    ordered = [sent[0]] + [facing(sent[k], k) for k in range(1, leaf_total)]
    up = (leaf_basis, transfer_one, transfer_two)
    matrices = up + (coupling_leaf, coupling_pair, coupling_quad)
    room = lambda arrays: [pltpu.SemaphoreType.DMA((len(arrays),))] + [pltpu.VMEM(m.shape, f32) for m in arrays]
    fetched = up + (side, sent[0])
    *held, side_held, kept = pl.pallas_call(
        fetch_kernel,
        out_shape=tuple(jax.ShapeDtypeStruct(m.shape, f32) for m in fetched),
        in_specs=[hbm] * len(fetched),
        out_specs=(vmem,) * len(fetched),
        scratch_shapes=room(fetched)[:1],
        compiler_params=small,
        name="fetch",
    )(*fetched)
    payload = pl.pallas_call(
        functools.partial(order_kernel, leaf_total, width),
        out_shape=jax.ShapeDtypeStruct((leaves, 4 * LANES), f32),
        in_specs=[vmem] * (leaf_total + 4),
        out_specs=vmem,
        compiler_params=small,
        name="order",
    )(kept, *ordered[1:], side_held, *held)
    gathered = nearby(payload)
    scratch = room(matrices) + [pltpu.VMEM((3 * leaves * reps, LANES), f32)] * 8
    scratch = scratch + [pltpu.VMEM((leaves, width, LANES), f32), pltpu.VMEM((width, LANES), f32)]
    scratch = scratch + [pltpu.VMEM((rank, LANES), f32)] * 3
    first = pl.pallas_call(
        functools.partial(first_kernel, len(gathered), near_count),
        out_shape=jax.ShapeDtypeStruct((leaves, 2 * LANES), f32),
        in_specs=[smem] + [vmem] * (len(gathered) + 1) + [hbm] * 6,
        out_specs=vmem,
        scratch_shapes=scratch,
        compiler_params=params,
        name="first",
    )(lists, *gathered, side, *matrices)
    later = nearby(first)
    second = pl.pallas_call(
        functools.partial(second_kernel, len(gathered), near_count),
        out_shape=(jax.ShapeDtypeStruct((capacity, 4 * LANES), f32),) * leaf_total,
        in_specs=[smem] + [vmem] * (2 * len(gathered) + 1) + [hbm] * 6,
        out_specs=(vmem,) * leaf_total,
        scratch_shapes=scratch,
        compiler_params=params,
        name="second",
    )(lists, *gathered, *later, side, *matrices)
    seconds = [second[0]] + [facing(second[k], k) for k in range(1, leaf_total)]
    last = sum(shard[:8, 2 * width :] for shard in seconds)
    lasts = [last] + [crossed(last, k) for k in range(1, reps)]
    second_image, first_image = pl.pallas_call(
        pick_kernel,
        out_shape=(jax.ShapeDtypeStruct((leaves, width), f32),) * 2,
        in_specs=[vmem] * (1 + leaf_total),
        out_specs=(vmem, vmem),
        compiler_params=small,
        name="pick",
    )(slots, *seconds)
    return pl.pallas_call(
        finish_kernel,
        out_shape=(jax.ShapeDtypeStruct((leaves, width), f32),) * 2,
        in_specs=[vmem] * (4 + reps),
        out_specs=(vmem, vmem),
        compiler_params=small,
        name="finish",
    )(start_point, start_residual, first_image, second_image, *lasts)


def solution(mesh):
    line = P(("groups", "leaf", "rep"))
    two = P(("groups", "leaf", "rep"), None)
    three = P(("groups", "leaf", "rep"), None, None)
    four = P(("groups", "leaf", "rep"), None, None, None)
    placed = (two, two, line, line, two, two, three, three, three, two, two, two, four, four, four, two)
    return jax.shard_map(body, mesh=mesh, in_specs=placed, out_specs=(two, two), check_vma=False)
```

```python
import functools

import jax
import jax.numpy as jnp
from jax import lax
from jax.experimental import pallas as pl
from jax.experimental.pallas import tpu as pltpu
from jax.sharding import PartitionSpec as P

PRECISE = lax.Precision.HIGHEST
JUMP = 0.5
SMOOTH_SQUARE = 0.01
KELVIN_DIAG = 2.2
EPSILON = 1e-06
LANES = 128
VMEM_LIMIT = 60 * 1024 * 1024


def lane_ids(rows):
    return lax.broadcasted_iota(jnp.int32, (rows, LANES), 1)


def columns_of(rows, count, column):
    lanes = lane_ids(rows)
    table = jnp.zeros((rows, LANES), jnp.float32)
    for g in range(count):
        table = jnp.where(lanes == g, column(g), table)
    return table


def lane_sum(value):
    return jnp.sum(value, axis=1, keepdims=True)


def expansions(masked, basis_ref, one_ref, two_ref, spare=None):
    leaves, rank = basis_ref.shape[0], basis_ref.shape[1]
    leaf_columns = columns_of(rank, leaves, lambda g: lane_sum(basis_ref[g] * masked[g : g + 1, :]))
    leaf_rows = leaf_columns.T[:leaves, :]
    pair_columns = columns_of(
        rank,
        leaves // 2,
        lambda c: lane_sum(
            one_ref[2 * c] * leaf_rows[2 * c : 2 * c + 1, :]
            + one_ref[2 * c + 1] * leaf_rows[2 * c + 1 : 2 * c + 2, :]
        ),
    )
    pair_rows = pair_columns.T[: leaves // 2, :]
    quad_columns = columns_of(
        rank,
        leaves // 4,
        lambda c: lane_sum(
            two_ref[2 * c] * pair_rows[2 * c : 2 * c + 1, :]
            + two_ref[2 * c + 1] * pair_rows[2 * c + 1 : 2 * c + 2, :]
        ),
    )
    quad_rows = quad_columns.T[: leaves // 4, :]
    if spare is None:
        spare = jnp.zeros((leaves - leaves // 2 - leaves // 4, rank), jnp.float32)
    upper = jnp.concatenate([pair_rows, quad_rows, spare], axis=0)
    return jnp.concatenate([leaf_rows, upper], axis=1)


def start_copies(sources, targets, sems):
    copies = [pltpu.make_async_copy(x, y, sems.at[i]) for i, (x, y) in enumerate(zip(sources, targets))]
    for copy in copies:
        copy.start()
    return copies


def exact_dot(left, right, dims=((1,), (0,))):
    return lax.dot_general(left, right, (dims, ((), ())), precision=PRECISE, preferred_element_type=jnp.float32)


def send_kernel(leaf_total, reps, order_ref, padding_ref, residual_ref, coords_ref, weight_ref, *refs):
    raw_lists, (slots_ref, side_ref, lists_ref), outs = refs[:4], refs[4:7], refs[7:]
    leaves, width = residual_ref.shape
    points = weight_ref.shape[1]
    leaf_index, rep_index = lax.axis_index("leaf"), lax.axis_index("rep")
    lists_ref[...] = jnp.zeros_like(lists_ref)
    for i, raw in enumerate(raw_lists):
        entries = raw[...]
        height = max(i - 1, 0)
        bits = (leaves >> height).bit_length() - 1
        owner = entries >> bits
        turned = (owner >> (reps.bit_length() - 1)) ^ leaf_index
        member = (owner & (reps - 1)) ^ rep_index
        side = (member & 1) * 3 + jnp.where(turned > 1, 2, turned)
        place = side * (reps // 2) + (member >> 1)
        row = place * leaves + (entries & ((1 << bits) - 1)) + (leaves // 2 if i == 3 else 0)
        lists_ref[8 * i : 8 * i + row.shape[0], 0 : row.shape[1]] = row
    capacity = side_ref.shape[0] - leaves
    order = order_ref[...]
    turned = (order >> ((leaves * reps).bit_length() - 1)) ^ leaf_index
    ids = lax.broadcasted_iota(jnp.int32, (8 * ((leaf_total + 7) // 8), leaves), 0)
    mine = (turned == ids).astype(jnp.float32)
    row, column = [lax.broadcasted_iota(jnp.int32, (leaves, leaves), i) for i in (0, 1)]
    padding = lane_sum(jnp.where(row == column, padding_ref[...].astype(jnp.float32), 0.0))
    point = lax.broadcasted_iota(jnp.int32, (leaves, width), 1) & (points - 1)
    mask = (point.astype(jnp.float32) < points - padding).astype(jnp.float32)
    weight = weight_ref[...] * mask[:, :points]
    side_ref[0:leaves, :] = jnp.concatenate([coords_ref[...], weight, mask, jnp.zeros((leaves, points), jnp.float32)], axis=1)
    rank = exact_dot(mine, (row < column).astype(jnp.float32))
    slot = lax.broadcasted_iota(jnp.int32, (capacity, leaves), 0).astype(jnp.float32)
    position = ((order & (leaves - 1)) + 1).astype(jnp.float32)
    slots = jnp.concatenate(
        [jnp.where(slot == rank[k : k + 1, :], mine[k : k + 1, :], 0.0) for k in range(leaf_total)], axis=0
    )
    slots_ref[...] = slots
    rows = exact_dot(slots, residual_ref[...])
    place = jnp.broadcast_to(lane_sum(slots * position), (leaf_total * capacity, 2 * LANES - width))
    payload = jnp.concatenate([rows, place], axis=1)
    side_ref[leaves:, :] = jnp.concatenate([payload[:capacity, :], jnp.zeros((capacity, 2 * LANES), jnp.float32)], axis=1)
    for k in range(1, leaf_total):
        outs[k - 1][...] = payload[k * capacity : (k + 1) * capacity, :]


def fetch_kernel(*refs):
    count = len(refs) // 2
    for copy in start_copies(refs[:count], refs[count:-1], refs[-1]):
        copy.wait()


def order_kernel(leaf_total, width, *refs):
    shards = refs[: leaf_total - 1]
    side_ref, basis_ref, one_ref, two_ref, out_ref = refs[leaf_total - 1 :]
    leaves = out_ref.shape[0]
    rows = jnp.concatenate([side_ref[leaves:, : 2 * LANES]] + [shard[...] for shard in shards], axis=0)
    ids = lax.broadcasted_iota(jnp.int32, (rows.shape[0], leaves), 1) + 1
    arrive = (rows[:, width : width + 1] == ids.astype(jnp.float32)).astype(jnp.float32)
    places = exact_dot(ids[:8, :].astype(jnp.float32), arrive, ((1,), (1,)))[:1, :]
    spare = [places[:, i : i + leaves] for i in range(0, arrive.shape[0], leaves)]
    spare = jnp.concatenate(spare + [jnp.zeros((8 - len(spare), leaves), jnp.float32)], axis=0)
    vector = exact_dot(arrive, rows, ((0,), (0,)))[:, :width]
    spread = expansions(side_ref[0:leaves, 256 : 256 + width] * vector, basis_ref, one_ref, two_ref, spare)
    out_ref[...] = jnp.concatenate([vector, spread, side_ref[0:leaves, :256]], axis=1)


def build_tables(place, geometry, vector, tables):
    rows = pl.ds(place * geometry.shape[0], geometry.shape[0])
    x_ref, y_ref, z_ref, u0_ref, u1_ref, u2_ref, leaf_ref, upper_ref = [ref.at[rows, :] for ref in tables]
    low = lane_ids(geometry.shape[0]) < 64
    swap = lambda v: pltpu.roll(v, 64, 1)
    first, second = geometry[:, :LANES], geometry[:, LANES:]
    first_swap, second_swap = swap(first), swap(second)
    x_ref[...] = jnp.where(low, first, first_swap)
    y_ref[...] = jnp.where(low, first_swap, first)
    z_ref[...] = jnp.where(low, second, second_swap)
    weight = jnp.where(low, second_swap, second)
    head, tail = vector[:, :LANES], vector[:, LANES:]
    head_swap, tail_swap = swap(head), swap(tail)
    u0_ref[...] = jnp.where(low, head, head_swap) * weight
    u1_ref[...] = jnp.where(low, head_swap, head) * weight
    u2_ref[...] = jnp.where(low, tail, tail_swap) * weight
    leaf_ref[...] = tail_swap
    upper_ref[...] = pltpu.roll(tail, 32, 1)


def near_field(lists_ref, near_count, target_ref, tables, out_ref):
    leaves, points = target_ref.shape[0], target_ref.shape[1] // 3
    low = lane_ids(8) < 64
    lanes = lane_ids(8)
    out_ref[...] = jnp.zeros_like(out_ref)

    def leaf_field(g):
        sources = []
        for k in range(0, near_count, 2):
            one, other = lists_ref[k, g], lists_ref[k + 1, g]
            values = [
                jnp.where(
                    low,
                    jnp.broadcast_to(ref[pl.ds(one, 1), :], (8, LANES)),
                    jnp.broadcast_to(ref[pl.ds(other, 1), :], (8, LANES)),
                )
                for ref in tables[:6]
            ]
            sources.append(values)
        for p in range(0, points, 8):
            tx, ty, tz = [target_ref[g, a * points + p : a * points + p + 8, :] for a in range(3)]
            direct = bent = None
            for x, y, z, u0, u1, u2 in sources:
                dx, dy, dz = tx - x, ty - y, tz - z
                inverse = lax.rsqrt(dx * dx + dy * dy + (dz * dz + SMOOTH_SQUARE))
                along = dx * u0 + dy * u1 + dz * u2
                cubic = (inverse * inverse) * (inverse * along)
                terms = [inverse * u0, inverse * u1, inverse * u2], [cubic * dx, cubic * dy, cubic * dz]
                direct = terms[0] if direct is None else [s + t for s, t in zip(direct, terms[0])]
                bent = terms[1] if bent is None else [s + t for s, t in zip(bent, terms[1])]
            sums = [KELVIN_DIAG * s + t for s, t in zip(direct, bent)]
            for a in range(3):
                rows = pl.ds(a * points + p, 8)
                out_ref[rows, :] = jnp.where(lanes == g, lane_sum(sums[a]), out_ref[rows, :])

    def some_leaves(step, carry):
        for u in range(8):
            leaf_field(step * 8 + u)
        return carry

    lax.fori_loop(0, leaves // 8, some_leaves, 0)


def coupled(entry, matrix_ref, table_ref, field_ref):
    count, partners, rank = matrix_ref.shape[:3]
    lanes = lane_ids(rank)
    step = 8

    def cluster_step(s, field):
        for u in range(step):
            t = s * step + u
            total = None
            for k in range(partners):
                row = table_ref[pl.ds(entry(t, k), 1), :][:, :rank]
                term = matrix_ref[t, k] * row
                total = term if total is None else total + term
            field = jnp.where(lanes == t, lane_sum(total), field)
        return field

    field_ref[...] = lax.fori_loop(0, count // step, cluster_step, jnp.zeros((rank, LANES), jnp.float32))


def rows_of(columns, matrix_ref, share):
    count = matrix_ref.shape[0]
    rows = []
    for c in range(count):
        column = columns[:, c // share : c // share + 1]
        rows.append(jnp.sum(matrix_ref[c] * column, axis=0, keepdims=True))
    return jnp.concatenate(rows, axis=0)


def columns_from_rows(rows):
    count, width = rows.shape
    padded = jnp.concatenate([rows, jnp.zeros((count, LANES - width), jnp.float32)], axis=1)
    full = jnp.concatenate([padded, jnp.zeros((LANES - count, LANES), jnp.float32)], axis=0)
    return full.T[:width, :]


def fill_targets(coords, target_ref):
    leaves, width = coords.shape
    padded = jnp.concatenate([coords, jnp.zeros((LANES - leaves, width), jnp.float32)], axis=0)
    columns = padded.T
    for g in range(leaves):
        target_ref[g] = jnp.broadcast_to(columns[:, g : g + 1], (width, LANES))


def operator(own, mask, lists_ref, near_count, copies, held, tables, scratch):
    basis_ref, one_ref, two_ref, c_leaf, c_pair, c_quad = held
    target_ref, near_out, f_leaf, f_pair, f_quad = scratch
    leaves = own.shape[0]
    near_field(lists_ref, near_count, target_ref, tables, near_out)
    for copy in copies:
        copy.wait()
    coupled(lambda t, k: lists_ref[24 + t, k], c_quad, tables[7], f_quad)
    coupled(lambda t, k: lists_ref[16 + k, t], c_pair, tables[7], f_pair)
    coupled(lambda t, k: lists_ref[8 + k, t], c_leaf, tables[6], f_leaf)
    total_pair = f_pair[...] + columns_from_rows(rows_of(f_quad[...], two_ref, 2))
    total_leaf = f_leaf[...] + columns_from_rows(rows_of(total_pair, one_ref, 2))
    far = rows_of(total_leaf, basis_ref, 1)
    near = near_out[...].T[:leaves, :]
    return mask * (JUMP * (mask * own) + near + far) + (1.0 - mask) * own


def total_of(value):
    return jnp.sum(jnp.sum(value, axis=1, keepdims=True), axis=0, keepdims=True)


def in_lanes(values):
    lanes = lane_ids(8)
    table = jnp.zeros((8, LANES), jnp.float32)
    for g, value in enumerate(values):
        table = jnp.where(lanes == g, value, table)
    return table


def first_kernel(parts, near_count, lists_ref, *refs):
    gathered, side_ref, sources = refs[:parts], refs[parts], refs[parts + 1 : parts + 7]
    out_ref, sems = refs[parts + 7 : parts + 9]
    held, tables, scratch = refs[parts + 9 : parts + 15], refs[parts + 15 : parts + 23], refs[parts + 23 :]
    width = held[0].shape[2]
    copies = start_copies(sources, held, sems)
    fill_targets(side_ref[0 : held[0].shape[0], :width], scratch[0])
    for i in range(parts):
        build_tables(i, gathered[i][:, 256:], gathered[i][:, :256], tables)
    own, mask = gathered[0][:, :width], side_ref[0 : held[0].shape[0], 256 : 256 + width]
    image = operator(own, mask, lists_ref, near_count, copies, held, tables, scratch)
    spread = expansions(mask * image, *held[:3])
    out_ref[...] = jnp.concatenate([image, spread], axis=1)


def second_kernel(parts, near_count, lists_ref, *refs):
    gathered, later, refs = refs[:parts], refs[parts : 2 * parts], refs[2 * parts :]
    side_ref, sources, outs, sems = refs[0], refs[1:7], refs[7:-20], refs[-20]
    held, tables, scratch = refs[-19:-13], refs[-13:-5], refs[-5:]
    width = held[0].shape[2]
    copies = start_copies(sources, held, sems)
    fill_targets(side_ref[0 : held[0].shape[0], :width], scratch[0])
    for i in range(parts):
        build_tables(i, gathered[i][:, 256:], later[i][...], tables)
    residual, own, mask = gathered[0][:, :width], later[0][:, :width], side_ref[0 : held[0].shape[0], 256 : 256 + width]
    image = operator(own, mask, lists_ref, near_count, copies, held, tables, scratch)
    pairs = ((residual, residual), (residual, own), (own, own), (residual, image), (own, image), (image, image))
    sums = in_lanes([total_of(x * y) for x, y in pairs])
    capacity = outs[0].shape[0]
    if capacity > 8:
        sums = jnp.concatenate([sums, jnp.zeros((capacity - 8, LANES), jnp.float32)], axis=0)
    leaves = own.shape[0]
    free = leaves // 2 + leaves // 4
    at = range(free, free + len(outs) * capacity // leaves)
    places = jnp.concatenate([gathered[0][i : i + 1, 2 * LANES - leaves : 2 * LANES] for i in at], axis=1)
    ids = lax.broadcasted_iota(jnp.int32, (leaves, places.shape[1]), 0) + 1
    arrive = (places == ids.astype(jnp.float32)).astype(jnp.float32)
    rows = exact_dot(arrive, jnp.concatenate([image, own], axis=1), ((0,), (0,)))
    for k, out_ref in enumerate(outs):
        out_ref[...] = jnp.concatenate([rows[k * capacity : (k + 1) * capacity, :], sums], axis=1)


def pick_kernel(slots_ref, *refs):
    shards, (second_ref, first_ref) = refs[:-2], refs[-2:]
    width = first_ref.shape[1]
    rows = jnp.concatenate([shard[...] for shard in shards], axis=0)
    found = exact_dot(slots_ref[...], rows[:, : 2 * width], ((0,), (0,)))
    second_ref[...] = found[:, :width]
    first_ref[...] = found[:, width:]


def finish_kernel(point_ref, residual_ref, first_ref, second_ref, *refs):
    next_point, next_residual = refs[-2:]
    sums = sum(ref[...] for ref in refs[:-2])
    rr, rw, ww, rv, wv, vv = [sums[0:1, j : j + 1] for j in range(6)]
    scale_square = rr + EPSILON
    scale = jnp.sqrt(scale_square)
    norm = rr / scale_square
    top_first = rw / scale_square
    rest_square = (ww - 2.0 * top_first * rw + top_first * top_first * rr) / scale_square
    along_image = (rv - top_first * rw) / scale_square
    rest_image = (wv - top_first * ww - top_first * (rv - top_first * rw)) / scale_square
    image_square = (vv - 2.0 * top_first * wv + top_first * top_first * ww) / scale_square
    rest_square = jnp.maximum(rest_square, 0.0)
    below_square = rest_square + EPSILON
    below_first = jnp.sqrt(below_square)
    top_second = along_image / below_first
    mid_second = rest_image / below_square
    image_square = image_square / below_square
    one_square = rest_square / below_square
    cross = (top_first - top_first * norm) / below_first
    below_second_square = (
        image_square
        - 2.0 * top_second * top_second
        - 2.0 * mid_second * mid_second
        + top_second * top_second * norm
        + mid_second * mid_second * one_square
        + 2.0 * top_second * mid_second * cross
        + EPSILON
    )
    gram_first = top_first * top_first + below_square
    gram_cross = top_first * top_second + below_first * mid_second
    gram_second = top_second * top_second + mid_second * mid_second + below_second_square
    determinant = gram_first * gram_second - gram_cross * gram_cross
    step_zero = scale * (gram_second * top_first - gram_cross * top_second) / determinant
    step_one = scale * (gram_first * top_second - gram_cross * top_first) / determinant
    residual, first = residual_ref[...], first_ref[...]
    rest = first - top_first * residual
    rest_image = second_ref[...] - top_first * first
    along_zero = step_zero / scale
    along_one = step_one / (scale * below_first)
    next_point[...] = point_ref[...] + along_zero * residual + along_one * rest
    next_residual[...] = residual - along_zero * first - along_one * rest_image


def body(
    start_point,
    start_residual,
    leaf_order,
    leaf_padding,
    point_coords,
    point_weights,
    leaf_basis,
    transfer_one,
    transfer_two,
    couple_leaf,
    couple_pair,
    couple_quad,
    coupling_leaf,
    coupling_pair,
    coupling_quad,
    near_lists,
):
    leaves, width = start_point.shape
    points = point_weights.shape[1]
    rank = leaf_basis.shape[1]
    leaf_total = lax.axis_size("leaf")
    reps = lax.axis_size("rep")
    f32 = jnp.float32
    vmem = pl.BlockSpec(memory_space=pltpu.VMEM)
    smem = pl.BlockSpec(memory_space=pltpu.SMEM)
    hbm = pl.BlockSpec(memory_space=pltpu.HBM)
    params = pltpu.CompilerParams(vmem_limit_bytes=VMEM_LIMIT)
    small = pltpu.CompilerParams(vmem_limit_bytes=VMEM_LIMIT // 4)

    def facing(value, turn):
        return lax.ppermute(value, "leaf", [(i, i ^ turn) for i in range(leaf_total)])

    def beside(value):
        other = [min(max(((i + 1) ^ 1) - 1, 0), leaf_total - 1) for i in range(leaf_total)]
        return lax.ppermute(value, "leaf", list(enumerate(other)))

    def crossed(value, step):
        return lax.ppermute(value, "rep", [(i, i ^ step) for i in range(reps)])

    def nearby(value):
        found = []
        others = [min(max(((i + 1) ^ 1) - 1, 0), leaf_total - 1) for i in range(leaf_total)]
        for along in (list(range(leaf_total)), [i ^ 1 for i in range(leaf_total)], others):
            for turn in range(0, reps, 2):
                pairs = [(i * reps + j, along[i] * reps + (j ^ turn)) for i in range(leaf_total) for j in range(reps)]
                moved = any(i != j for i, j in pairs)
                found.append(lax.ppermute(value, ("leaf", "rep"), pairs) if moved else value)
        return found + [crossed(part, 1) for part in found]

    near_count = near_lists.shape[1]
    raw_lists = (near_lists.T, couple_leaf.T, couple_pair.T, couple_quad)

    capacity = max(8, 2 * leaves // leaf_total)
    sent = pl.pallas_call(
        functools.partial(send_kernel, leaf_total, reps),
        out_shape=(
            jax.ShapeDtypeStruct((leaf_total * capacity, leaves), f32),
            jax.ShapeDtypeStruct((leaves + capacity, 4 * LANES), f32),
            jax.ShapeDtypeStruct((32, leaves), jnp.int32),
        )
        + (jax.ShapeDtypeStruct((capacity, 2 * LANES), f32),) * (leaf_total - 1),
        in_specs=[vmem] * 9,
        out_specs=(vmem,) * (leaf_total + 2),
        compiler_params=params,
        name="send",
    )(
        leaf_order.reshape(1, leaves),
        leaf_padding.reshape(1, leaves),
        start_residual,
        point_coords,
        point_weights,
        *raw_lists,
    )
    slots, side, lists, *sent = sent
    ordered = [facing(sent[k - 1], k) for k in range(1, leaf_total)]
    up = (leaf_basis, transfer_one, transfer_two)
    matrices = up + (coupling_leaf, coupling_pair, coupling_quad)
    room = lambda arrays: [pltpu.SemaphoreType.DMA((len(arrays),))] + [pltpu.VMEM(m.shape, f32) for m in arrays]
    fetched = up + (side,)
    *held, side_held = pl.pallas_call(
        fetch_kernel,
        out_shape=tuple(jax.ShapeDtypeStruct(m.shape, f32) for m in fetched),
        in_specs=[hbm] * len(fetched),
        out_specs=(vmem,) * len(fetched),
        scratch_shapes=room(fetched)[:1],
        compiler_params=small,
        name="fetch",
    )(*fetched)
    payload = pl.pallas_call(
        functools.partial(order_kernel, leaf_total, width),
        out_shape=jax.ShapeDtypeStruct((leaves, 4 * LANES), f32),
        in_specs=[vmem] * (leaf_total + 3),
        out_specs=vmem,
        compiler_params=small,
        name="order",
    )(*ordered, side_held, *held)
    gathered = nearby(payload)
    scratch = room(matrices) + [pltpu.VMEM((3 * leaves * reps, LANES), f32)] * 8
    scratch = scratch + [pltpu.VMEM((leaves, width, LANES), f32), pltpu.VMEM((width, LANES), f32)]
    scratch = scratch + [pltpu.VMEM((rank, LANES), f32)] * 3
    first = pl.pallas_call(
        functools.partial(first_kernel, len(gathered), near_count),
        out_shape=jax.ShapeDtypeStruct((leaves, 2 * LANES), f32),
        in_specs=[smem] + [vmem] * (len(gathered) + 1) + [hbm] * 6,
        out_specs=vmem,
        scratch_shapes=scratch,
        compiler_params=params,
        name="first",
    )(lists, *gathered, side, *matrices)
    later = nearby(first)
    second = pl.pallas_call(
        functools.partial(second_kernel, len(gathered), near_count),
        out_shape=(jax.ShapeDtypeStruct((capacity, 4 * LANES), f32),) * leaf_total,
        in_specs=[smem] + [vmem] * (2 * len(gathered) + 1) + [hbm] * 6,
        out_specs=(vmem,) * leaf_total,
        scratch_shapes=scratch,
        compiler_params=params,
        name="second",
    )(lists, *gathered, *later, side, *matrices)
    seconds = [second[0]] + [facing(second[k], k) for k in range(1, leaf_total)]
    last = sum(shard[:8, 2 * width :] for shard in seconds)
    lasts = [last] + [crossed(last, k) for k in range(1, reps)]
    second_image, first_image = pl.pallas_call(
        pick_kernel,
        out_shape=(jax.ShapeDtypeStruct((leaves, width), f32),) * 2,
        in_specs=[vmem] * (1 + leaf_total),
        out_specs=(vmem, vmem),
        compiler_params=small,
        name="pick",
    )(slots, *seconds)
    return pl.pallas_call(
        finish_kernel,
        out_shape=(jax.ShapeDtypeStruct((leaves, width), f32),) * 2,
        in_specs=[vmem] * (4 + reps),
        out_specs=(vmem, vmem),
        compiler_params=small,
        name="finish",
    )(start_point, start_residual, first_image, second_image, *lasts)


def solution(mesh):
    line = P(("groups", "leaf", "rep"))
    two = P(("groups", "leaf", "rep"), None)
    three = P(("groups", "leaf", "rep"), None, None)
    four = P(("groups", "leaf", "rep"), None, None, None)
    placed = (two, two, line, line, two, two, three, three, three, two, two, two, four, four, four, two)
    return jax.shard_map(body, mesh=mesh, in_specs=placed, out_specs=(two, two), check_vma=False)
```
